32 devices in a mesh: seq: 8 (over y, x, core), mp: 4 (over z).
Axes of the slice: x: 2, y: 2, z: 4, core: 2. Of those that a mesh axis runs over, the one named last changes fastest.
Arguments:
- projected: bfloat16 [3, 8192, 1024], P(None, 'mp', 'seq'), may hold values from -6 to 6
- short_taps: float32 [3, 3, 8192], replicated, may hold values from -4 to 4
- skip_gain: float32 [8192], replicated, may hold values from -4 to 4
- residue: float32 [2048, 16], P('seq'), may hold values from -4 to 4
- decay_rate: float32 [2048, 16], P('seq'), may hold values from 0.00048828125 to 0.05
Outputs:
- gated: bfloat16 [8192, 1024], P('mp', 'seq')
The draws below stay inside these ranges and needn't reach their ends.
All inputs are finite; a program needn't handle non-finite values.
Results may differ from the reference program's by a relative error of at most 0.012.
Values may be sent and summed in bfloat16 or wider, within the bound.
A program may use at most 128 MiB of HBM per device.

```python
import math
import jax
import jax.numpy as jnp
from jax import lax

C = 8192
FILTERS = 2048
STATE = 16
SEQ = 1024


def levels(stream_key, shape, pieces, low, top_value):
    factor_of, own = 1.0, jax.random.fold_in(stream_key, 6)
    for axis_at, blocks in pieces:
        draws = jnp.exp(jax.random.uniform(jax.random.fold_in(own, axis_at), (blocks,), jnp.float32, low / len(pieces), top_value / len(pieces)))
        factor_of = factor_of * jnp.repeat(draws, shape[axis_at] // blocks).reshape([-1 if axis == axis_at else 1 for axis in range(len(shape))])
    return factor_of


def bell_draw(stream_key, dims, width, reach, cuts=(), held_as=jnp.bfloat16):
    drawn = width * jax.random.normal(stream_key, dims, jnp.float32)
    if cuts:
        drawn = drawn * levels(stream_key, dims, cuts, -0.22, 0.18)
    return jnp.clip(drawn, -reach, reach).astype(held_as)


def setup_inputs(seed: int = 0) -> dict:
    seeds = jax.random.split(jax.random.key(seed), 6)
    return {
        "projected": bell_draw(seeds[0], (3, C, SEQ), 1.0, 6.0, ((1, 4), (2, 8))),
        "short_taps": bell_draw(seeds[1], (3, 3, C), 0.6, 4.0, (), jnp.float32),
        "skip_gain": bell_draw(seeds[2], (C,), 1.0, 4.0, (), jnp.float32),
        "residue": bell_draw(seeds[3], (FILTERS, STATE), 0.5, 4.0, ((0, 8),), jnp.float32),
        "decay_rate": jnp.clip(jnp.exp(math.log(0.05) - 4.6288867 * jax.random.uniform(seeds[4], (FILTERS, STATE), jnp.float32) ** levels(seeds[4], (FILTERS, STATE), ((0, 8),), -0.2, 0.2)), 0.00048828125, 0.05),
    }


def filter_kernel(residue_block, rate_block, length):
    positions = jnp.arange(length, dtype=jnp.float32)
    kernel = jnp.zeros((residue_block.shape[0], length), jnp.float32)
    for state_index in range(STATE):
        weight = residue_block[:, state_index] * jnp.sqrt(rate_block[:, state_index])
        kernel = kernel + weight[:, None] * jnp.exp(-rate_block[:, state_index][:, None] * positions[None, :])
    return kernel

def reference(projected, short_taps, skip_gain, residue, decay_rate):
    channels = projected.shape[1]
    length = projected.shape[2]
    block_size = math.gcd(512, FILTERS)
    block_count = channels // block_size

    def one_block(block_index):
        offset = (block_index * block_size).astype(jnp.int32)
        values = lax.dynamic_slice_in_dim(projected, offset, block_size, 1).astype(jnp.float32)
        tap_block = lax.dynamic_slice_in_dim(short_taps, offset, block_size, 2)
        padded = jnp.pad(values, ((0, 0), (0, 0), (2, 0)))
        mixed = tap_block[0][:, :, None] * values + tap_block[1][:, :, None] * padded[:, :, 1:-1] + tap_block[2][:, :, None] * padded[:, :, :-2]
        product = (mixed[1] * mixed[2]).astype(jnp.bfloat16)
        filter_start = (offset % FILTERS).astype(jnp.int32)
        residue_block = lax.dynamic_slice_in_dim(residue, filter_start, block_size, 0)
        rate_block = lax.dynamic_slice_in_dim(decay_rate, filter_start, block_size, 0)
        kernel = filter_kernel(residue_block, rate_block, length)
        spectrum = jnp.fft.rfft(product.astype(jnp.float32), n=2 * length) * jnp.fft.rfft(kernel, n=2 * length)
        long_part = jnp.fft.irfft(spectrum, n=2 * length)[:, :length].astype(jnp.bfloat16)
        skip_block = lax.dynamic_slice_in_dim(skip_gain, offset, block_size, 0)
        total = long_part.astype(jnp.float32) + skip_block[:, None] * product.astype(jnp.float32)
        return (mixed[0] * total).astype(jnp.bfloat16)
    gated = lax.map(one_block, jnp.arange(block_count, dtype=jnp.int32))
    return gated.reshape(channels, length)
```

```python
import functools

import jax
import jax.numpy as jnp
from jax import lax
from jax.experimental import pallas as pl
from jax.experimental.pallas import tpu as pltpu
from jax.sharding import PartitionSpec as P

MESH = pl.DeviceIdType.MESH
LANES = 128
ROWS = 8


def rows_of(first, count=ROWS):
    return pl.ds(pl.multiple_of(first, ROWS), count)


def kernel(
    seq_count,
    modes,
    half_count,
    length,
    filters,
    projected,
    taps_hbm,
    skip_hbm,
    residue,
    rate,
    out,
    streams,
    taps_raw,
    skip,
    taps,
    laid,
    product,
    mixed_q,
    local,
    own_params,
    params,
    rates,
    weights,
    decay,
    block_decay,
    halo_out,
    halo_in,
    own_state,
    states,
    carry,
    in_sem,
    tap_sem,
    param_send,
    param_recv,
    halo_send,
    halo_recv,
    state_send,
    state_recv,
):
    me = lax.axis_index("seq")
    group = lax.axis_index("mp")
    block_count = half_count * ROWS
    width = block_count * LANES
    half_rows = length * ROWS

    in_copies = [
        pltpu.make_async_copy(projected.at[s], streams.at[s], in_sem.at[s]) for s in range(3)
    ]
    tap_copy = pltpu.make_async_copy(
        taps_hbm.at[:, :, pl.ds(pl.multiple_of(group * width, LANES), width)],
        taps_raw,
        tap_sem.at[0],
    )
    skip_copy = pltpu.make_async_copy(
        skip_hbm.at[rows_of(group * block_count, block_count)], skip, tap_sem.at[1]
    )
    for copy in in_copies:
        copy.start()
    tap_copy.start()
    skip_copy.start()

    barrier = pltpu.get_barrier_semaphore()

    def greet(step, _):
        peer = lax.rem(me + step, seq_count)
        pl.semaphore_signal(barrier, inc=1, device_id={"seq": peer}, device_id_type=MESH)
        return 0

    lax.fori_loop(1, seq_count, greet, 0)
    own_params[0] = rate[...]
    own_params[1] = residue[...] * jnp.sqrt(rate[...])
    params[me] = own_params[...]
    pl.semaphore_wait(barrier, seq_count - 1)

    def param_copy(step):
        peer = lax.rem(me + step, seq_count)
        return pltpu.make_async_remote_copy(
            src_ref=own_params,
            dst_ref=params.at[me],
            send_sem=param_send.at[step],
            recv_sem=param_recv.at[step],
            device_id={"seq": peer},
            device_id_type=MESH,
        )

    def send_params(step, _):
        param_copy(step).start()
        return 0

    lax.fori_loop(1, seq_count, send_params, 0)

    eye = (
        lax.broadcasted_iota(jnp.int32, (LANES, LANES), 0)
        == lax.broadcasted_iota(jnp.int32, (LANES, LANES), 1)
    ).astype(jnp.bfloat16)
    across = (((1,), (1,)), ((), ()))
    for s in range(3):
        in_copies[s].wait()
        for pair in range(block_count // 2):
            turned = lax.dot_general(
                eye,
                streams[s, pair * 256 : pair * 256 + 256, :],
                across,
                preferred_element_type=jnp.float32,
            )
            for side in range(2):
                half, row = divmod(pair * 2 + side, ROWS)
                laid[pl.ds((s * half_count + half) * half_rows + row, length, stride=ROWS), :] = (
                    turned[:, side * LANES : (side + 1) * LANES]
                )

    def laid_row(s, half, t):
        return laid[rows_of((s * half_count + half) * half_rows + t * ROWS), :]

    for s in range(3):
        for back in range(2):
            pieces = [laid_row(s, half, length - 2 + back) for half in range(half_count)]
            halo_out[s * 2 + back] = jnp.concatenate(pieces, axis=0).astype(jnp.bfloat16)

    halo_copy = pltpu.make_async_remote_copy(
        src_ref=halo_out,
        dst_ref=halo_in,
        send_sem=halo_send,
        recv_sem=halo_recv,
        device_id={"seq": lax.rem(me + 1, seq_count)},
        device_id_type=MESH,
    )

    @pl.when(me < seq_count - 1)
    def _():
        halo_copy.start()

    tap_copy.wait()
    skip_copy.wait()
    for lag in range(3):
        for s in range(3):
            for block in range(block_count):
                taps[lag * 3 + s, block : block + 1, :] = taps_raw[
                    lag, s : s + 1, block * LANES : (block + 1) * LANES
                ]

    def tap_rows(half):
        return [
            [taps[lag * 3 + s, half * ROWS : (half + 1) * ROWS, :] for lag in range(3)]
            for s in range(3)
        ]

    def put_mixed(half, t, now, before, earlier, tap):
        q, k, v = [
            tap[s][0] * now[s] + tap[s][1] * before[s] + tap[s][2] * earlier[s] for s in range(3)
        ]
        at = rows_of(half * half_rows + t * ROWS)
        mixed_q[at, :] = q
        product[at, :] = (k * v).astype(jnp.bfloat16).astype(jnp.float32)

    for half in range(half_count):
        tap = tap_rows(half)

        def mix(t, past, half=half, tap=tap):
            before, earlier = past
            now = [laid_row(s, half, t) for s in range(3)]
            put_mixed(half, t, now, before, earlier, tap)
            return now, before

        first = [[laid_row(s, half, t) for s in range(3)] for t in range(2)]
        lax.fori_loop(2, length, mix, (first[1], first[0]), unroll=6)

    @pl.when(me > 0)
    def _():
        halo_copy.wait_recv()

    @pl.when(me == 0)
    def _():
        halo_in[...] = jnp.zeros(halo_in.shape, halo_in.dtype)

    for half in range(half_count):
        tap = tap_rows(half)
        past = [
            [
                halo_in[s * 2 + back].astype(jnp.float32)[half * ROWS : (half + 1) * ROWS]
                for s in range(3)
            ]
            for back in range(2)
        ]
        first = [[laid_row(s, half, t) for s in range(3)] for t in range(2)]
        put_mixed(half, 0, first[0], past[1], past[0], tap)
        put_mixed(half, 1, first[1], first[0], past[1], tap)

    def take_params(step, _):
        param_copy(step).wait_recv()
        return 0

    lax.fori_loop(1, seq_count, take_params, 0)
    for block in range(block_count):
        half, row = divmod(block, ROWS)
        for kind, target in ((0, rates), (1, weights)):
            if filters >= LANES:
                per = filters // LANES
                lane = (block % per) * LANES
                piece = params[block // per, kind, :, lane : lane + LANES]
            else:
                per = LANES // filters
                piece = jnp.concatenate(
                    [params[block * per + part, kind] for part in range(per)], axis=1
                )
            target[pl.ds(half * modes * ROWS + row, modes, stride=ROWS), :] = piece
    decay[...] = jnp.exp(-rates[...])
    block_decay[...] = jnp.exp(-float(length) * rates[...])

    def of_modes(ref, half):
        first = half * modes * ROWS
        return [ref[first + n * ROWS : first + (n + 1) * ROWS, :] for n in range(modes)]

    def state_copy(half, step):
        peer = lax.rem(me + step, seq_count)
        return pltpu.make_async_remote_copy(
            src_ref=own_state.at[half],
            dst_ref=states.at[me, half],
            send_sem=state_send.at[half, step],
            recv_sem=state_recv.at[half, step],
            device_id={"seq": peer},
            device_id_type=MESH,
        )

    for half in range(half_count):
        rate_of = of_modes(decay, half)

        def gather_state(t, held, half=half, rate_of=rate_of):
            value = product[rows_of(half * half_rows + t * ROWS), :]
            return [rate_of[n] * held[n] + value for n in range(modes)]

        held = lax.fori_loop(
            0,
            length,
            gather_state,
            [jnp.zeros((ROWS, LANES), jnp.float32)] * modes,
            unroll=8,
        )
        own_state[half] = jnp.concatenate(held, axis=0).astype(jnp.bfloat16)

        def send_state(step, _, half=half):
            state_copy(half, step).start()
            return 0

        lax.fori_loop(1, seq_count - me, send_state, 0)

    for half in range(half_count):
        rate_of = of_modes(decay, half)
        weight_of = of_modes(weights, half)

        def convolve(t, held, half=half, rate_of=rate_of, weight_of=weight_of):
            at = rows_of(half * half_rows + t * ROWS)
            value = product[at, :]
            held = [rate_of[n] * held[n] + value for n in range(modes)]
            local[at, :] = tree_sum([weight_of[n] * held[n] for n in range(modes)])
            return held

        lax.fori_loop(
            0, length, convolve, [jnp.zeros((ROWS, LANES), jnp.float32)] * modes, unroll=4
        )

    for half in range(half_count):
        mode_rows = modes * ROWS
        first = half * mode_rows
        carry[...] = jnp.zeros(carry.shape, jnp.float32)

        def take_state(sender, _, half=half, first=first):
            state_copy(half, me - sender).wait_recv()
            carry[...] = carry[...] * block_decay[first : first + mode_rows, :] + states[
                sender, half
            ].astype(jnp.float32)
            return 0

        lax.fori_loop(0, me, take_state, 0)
        carry[...] = carry[...] * weights[first : first + mode_rows, :]
        rate_of = of_modes(decay, half)
        skip_here = skip[half * ROWS : (half + 1) * ROWS, :]

        def finish(t, held, half=half, rate_of=rate_of, skip_here=skip_here):
            at = rows_of(half * half_rows + t * ROWS)
            held = [rate_of[n] * held[n] for n in range(modes)]
            long_part = (local[at, :] + tree_sum(held)).astype(jnp.bfloat16).astype(jnp.float32)
            local[at, :] = mixed_q[at, :] * (long_part + skip_here * product[at, :])
            return held

        lax.fori_loop(0, length, finish, of_modes(carry, 0), unroll=4)
        for row in range(ROWS):
            gated = local[pl.ds(half * half_rows + row, length, stride=ROWS), :].astype(jnp.bfloat16)
            first_channel = (half * ROWS + row) * LANES
            out[first_channel : first_channel + LANES, :] = lax.dot_general(
                eye, gated, across, preferred_element_type=jnp.float32
            ).astype(jnp.bfloat16)

    def drain_params(step, _):
        param_copy(step).wait_send()
        return 0

    lax.fori_loop(1, seq_count, drain_params, 0)

    @pl.when(me < seq_count - 1)
    def _():
        halo_copy.wait_send()

    def drain_states(step, _):
        for half in range(half_count):
            state_copy(half, step).wait_send()
        return 0

    lax.fori_loop(1, seq_count - me, drain_states, 0)


def tree_sum(terms):
    while len(terms) > 1:
        terms = [terms[i] + terms[i + 1] for i in range(0, len(terms), 2)]
    return terms[0]


def body(projected, short_taps, skip_gain, residue, decay_rate):
    seq_count = lax.axis_size("seq")
    _, width, length = projected.shape
    filters, modes = residue.shape
    block_count = width // LANES
    half_count = block_count // ROWS
    call = functools.partial(kernel, seq_count, modes, half_count, length, filters)
    vmem = pl.BlockSpec(memory_space=pltpu.VMEM)
    anywhere = pl.BlockSpec(memory_space=pl.ANY)
    mode_rows = modes * ROWS
    f32, bf16 = jnp.float32, jnp.bfloat16
    dma = pltpu.SemaphoreType.DMA
    return pl.pallas_call(
        call,
        out_shape=jax.ShapeDtypeStruct((width, length), bf16),
        in_specs=[anywhere, anywhere, anywhere, vmem, vmem],
        out_specs=vmem,
        scratch_shapes=[
            pltpu.VMEM((3, width, length), bf16),
            pltpu.VMEM((3, 3, width), f32),
            pltpu.VMEM((block_count, LANES), f32),
            pltpu.VMEM((9, block_count, LANES), f32),
            pltpu.VMEM((3 * length * block_count, LANES), f32),
            pltpu.VMEM((length * block_count, LANES), f32),
            pltpu.VMEM((length * block_count, LANES), f32),
            pltpu.VMEM((length * block_count, LANES), f32),
            pltpu.VMEM((2, modes, filters), f32),
            pltpu.VMEM((seq_count, 2, modes, filters), f32),
            pltpu.VMEM((half_count * mode_rows, LANES), f32),
            pltpu.VMEM((half_count * mode_rows, LANES), f32),
            pltpu.VMEM((half_count * mode_rows, LANES), f32),
            pltpu.VMEM((half_count * mode_rows, LANES), f32),
            pltpu.VMEM((6, block_count, LANES), bf16),
            pltpu.VMEM((6, block_count, LANES), bf16),
            pltpu.VMEM((half_count, mode_rows, LANES), bf16),
            pltpu.VMEM((seq_count, half_count, mode_rows, LANES), bf16),
            pltpu.VMEM((mode_rows, LANES), f32),
            dma((3,)),
            dma((2,)),
            dma((seq_count,)),
            dma((seq_count,)),
            dma,
            dma,
            dma((half_count, seq_count)),
            dma((half_count, seq_count)),
        ],
        compiler_params=pltpu.CompilerParams(
            collective_id=0, has_side_effects=True, vmem_limit_bytes=40 * 1024 * 1024
        ),
    )(
        projected,
        short_taps,
        skip_gain.reshape(skip_gain.shape[0] // LANES, LANES),
        residue.T,
        decay_rate.T,
    )


def solution(mesh):
    in_specs = (P(None, "mp", "seq"), P(), P(), P("seq", None), P("seq", None))
    out_specs = P("mp", "seq")
    return jax.shard_map(body, mesh=mesh, in_specs=in_specs, out_specs=out_specs, check_vma=False)
```

```python
import functools

import jax
import jax.numpy as jnp
from jax import lax
from jax.experimental import pallas as pl
from jax.experimental.pallas import tpu as pltpu
from jax.sharding import PartitionSpec as P

MESH = pl.DeviceIdType.MESH
LANES = 128
ROWS = 8


def rows_of(first, count=ROWS):
    return pl.ds(pl.multiple_of(first, ROWS), count)


def kernel(
    seq_count,
    modes,
    half_count,
    length,
    filters,
    projected,
    taps_hbm,
    skip_hbm,
    residue_hbm,
    rate_hbm,
    out,
    residue,
    rate,
    streams,
    taps_raw,
    skip,
    taps,
    laid,
    product,
    mixed_q,
    local,
    own_params,
    params,
    rates,
    weights,
    decay,
    block_decay,
    pair_decay,
    halo_out,
    halo_in,
    own_state,
    mate_state,
    pair_state,
    states,
    carry,
    staged,
    in_sem,
    out_sem,
    tap_sem,
    param_send,
    param_recv,
    halo_send,
    halo_recv,
    mate_send,
    mate_recv,
    state_send,
    state_recv,
):
    me = lax.axis_index("seq")
    group = lax.axis_index("mp")
    block_count = half_count * ROWS
    width = block_count * LANES
    half_rows = length * ROWS
    mode_rows = modes * ROWS
    side = lax.rem(me, 2)
    pair = lax.div(me, 2)
    pair_count = seq_count // 2
    mate = me + 1 - 2 * side

    in_copies = [
        pltpu.make_async_copy(projected.at[s], streams.at[s], in_sem.at[s]) for s in range(3)
    ]
    tap_copy = pltpu.make_async_copy(
        taps_hbm.at[:, :, pl.ds(pl.multiple_of(group * width, LANES), width)],
        taps_raw,
        tap_sem.at[0],
    )
    skip_copy = pltpu.make_async_copy(
        skip_hbm.at[rows_of(group * block_count, block_count)], skip, tap_sem.at[1]
    )
    rate_copy = pltpu.make_async_copy(rate_hbm, rate, tap_sem.at[2])
    residue_copy = pltpu.make_async_copy(residue_hbm, residue, tap_sem.at[3])
    rate_copy.start()
    residue_copy.start()
    for copy in in_copies:
        copy.start()
    tap_copy.start()
    skip_copy.start()

    barrier = pltpu.get_barrier_semaphore()

    def greet(step, _):
        peer = lax.rem(me + step, seq_count)
        pl.semaphore_signal(barrier, inc=1, device_id={"seq": peer}, device_id_type=MESH)
        return 0

    lax.fori_loop(1, seq_count, greet, 0)
    rate_copy.wait()
    residue_copy.wait()
    own_params[0] = rate[...]
    own_params[1] = residue[...] * jnp.sqrt(rate[...])
    params[me] = own_params[...]
    pl.semaphore_wait(barrier, seq_count - 1)

    def param_copy(kind, step):
        peer = lax.rem(me + step, seq_count)
        return pltpu.make_async_remote_copy(
            src_ref=own_params.at[kind],
            dst_ref=params.at[me, kind],
            send_sem=param_send.at[kind, step],
            recv_sem=param_recv.at[kind, step],
            device_id={"seq": peer},
            device_id_type=MESH,
        )

    def send_params(kind):
        def send(step, _):
            param_copy(kind, step).start()
            return 0

        lax.fori_loop(1, seq_count, send, 0)

    send_params(0)

    eye = (
        lax.broadcasted_iota(jnp.int32, (LANES, LANES), 0)
        == lax.broadcasted_iota(jnp.int32, (LANES, LANES), 1)
    ).astype(jnp.bfloat16)
    across = (((1,), (1,)), ((), ()))
    for s in range(3):
        in_copies[s].wait()
        for couple in range(block_count // 2):
            turned = lax.dot_general(
                eye,
                streams[s, couple * 256 : couple * 256 + 256, :],
                across,
                preferred_element_type=jnp.float32,
            )
            for part in range(2):
                half, row = divmod(couple * 2 + part, ROWS)
                laid[pl.ds((s * half_count + half) * half_rows + row, length, stride=ROWS), :] = (
                    turned[:, part * LANES : (part + 1) * LANES]
                )

    def laid_row(s, half, t):
        return laid[rows_of((s * half_count + half) * half_rows + t * ROWS), :]

    for s in range(3):
        for back in range(2):
            pieces = [laid_row(s, half, length - 2 + back) for half in range(half_count)]
            halo_out[s * 2 + back] = jnp.concatenate(pieces, axis=0).astype(jnp.bfloat16)

    halo_copy = pltpu.make_async_remote_copy(
        src_ref=halo_out,
        dst_ref=halo_in,
        send_sem=halo_send,
        recv_sem=halo_recv,
        device_id={"seq": lax.rem(me + 1, seq_count)},
        device_id_type=MESH,
    )

    @pl.when(me < seq_count - 1)
    def _():
        halo_copy.start()

    send_params(1)
    tap_copy.wait()
    skip_copy.wait()
    for lag in range(3):
        for s in range(3):
            for block in range(block_count):
                taps[lag * 3 + s, block : block + 1, :] = taps_raw[
                    lag, s : s + 1, block * LANES : (block + 1) * LANES
                ]

    def tap_rows(half):
        return [
            [taps[lag * 3 + s, half * ROWS : (half + 1) * ROWS, :] for lag in range(3)]
            for s in range(3)
        ]

    def put_mixed(half, t, now, before, earlier, tap):
        q, k, v = [
            tap[s][0] * now[s] + tap[s][1] * before[s] + tap[s][2] * earlier[s] for s in range(3)
        ]
        at = rows_of(half * half_rows + t * ROWS)
        mixed_q[at, :] = q
        product[at, :] = (k * v).astype(jnp.bfloat16).astype(jnp.float32)

    for half in range(half_count):
        tap = tap_rows(half)

        def mix(t, past, half=half, tap=tap):
            before, earlier = past
            now = [laid_row(s, half, t) for s in range(3)]
            put_mixed(half, t, now, before, earlier, tap)
            return now, before

        first = [[laid_row(s, half, t) for s in range(3)] for t in range(2)]
        lax.fori_loop(2, length, mix, (first[1], first[0]), unroll=6)

    @pl.when(me > 0)
    def _():
        halo_copy.wait_recv()

    @pl.when(me == 0)
    def _():
        halo_in[...] = jnp.zeros(halo_in.shape, halo_in.dtype)

    for half in range(half_count):
        tap = tap_rows(half)
        past = [
            [
                halo_in[s * 2 + back].astype(jnp.float32)[half * ROWS : (half + 1) * ROWS]
                for s in range(3)
            ]
            for back in range(2)
        ]
        first = [[laid_row(s, half, t) for s in range(3)] for t in range(2)]
        put_mixed(half, 0, first[0], past[1], past[0], tap)
        put_mixed(half, 1, first[1], first[0], past[1], tap)

    def take_params(kind, target):
        def take(step, _):
            param_copy(kind, step).wait_recv()
            return 0

        lax.fori_loop(1, seq_count, take, 0)
        for block in range(block_count):
            half, row = divmod(block, ROWS)
            if filters >= LANES:
                per = filters // LANES
                lane = (block % per) * LANES
                piece = params[block // per, kind, :, lane : lane + LANES]
            else:
                per = LANES // filters
                piece = jnp.concatenate(
                    [params[block * per + part, kind] for part in range(per)], axis=1
                )
            target[pl.ds(half * mode_rows + row, modes, stride=ROWS), :] = piece

    take_params(0, rates)
    decay[...] = jnp.exp(-rates[...])

    def of_modes(ref, half):
        first = half * mode_rows
        return [ref[rows_of(first + n * ROWS), :] for n in range(modes)]

    def find_state(half):
        rate_of = of_modes(decay, half)

        def gather_state(t, held):
            value = product[rows_of(half * half_rows + t * ROWS), :]
            return [rate_of[n] * held[n] + value for n in range(modes)]

        held = lax.fori_loop(
            0,
            length,
            gather_state,
            [jnp.zeros((ROWS, LANES), jnp.float32)] * modes,
            unroll=8,
        )
        own_state[half] = jnp.concatenate(held, axis=0).astype(jnp.bfloat16)

    def mate_copy(half):
        return pltpu.make_async_remote_copy(
            src_ref=own_state.at[half],
            dst_ref=mate_state.at[half],
            send_sem=mate_send.at[half],
            recv_sem=mate_recv.at[half],
            device_id={"seq": mate},
            device_id_type=MESH,
        )

    find_state(1 - side)
    mate_copy(1 - side).start()
    block_decay[...] = jnp.exp(-float(length) * rates[...])
    pair_decay[...] = block_decay[...] * block_decay[...]
    find_state(side)

    @pl.when(side == 0)
    def _():
        mate_copy(0).start()

    def state_copy(later, target_side):
        return pltpu.make_async_remote_copy(
            src_ref=pair_state,
            dst_ref=states.at[pair, side],
            send_sem=state_send.at[later, target_side],
            recv_sem=state_recv.at[pair, side],
            device_id={"seq": 2 * later + target_side},
            device_id_type=MESH,
        )

    def for_later(action):
        def step(later, _):
            for target_side in range(2):
                action(state_copy(later, target_side))
            return 0

        lax.fori_loop(pair + 1, pair_count, step, 0)

    mate_copy(side).wait_recv()
    own_part = own_state[side].astype(jnp.float32)
    mate_part = mate_state[side].astype(jnp.float32)
    scale = block_decay[rows_of(side * mode_rows, mode_rows), :]
    even = jnp.where(side == 0, own_part, mate_part)
    odd = jnp.where(side == 0, mate_part, own_part)
    pair_state[...] = (scale * even + odd).astype(jnp.bfloat16)
    for_later(lambda copy: copy.start())
    take_params(1, weights)

    for half in range(half_count):
        rate_of = of_modes(decay, half)
        weight_of = of_modes(weights, half)

        def convolve(t, held, half=half, rate_of=rate_of, weight_of=weight_of):
            at = rows_of(half * half_rows + t * ROWS)
            value = product[at, :]
            held = [rate_of[n] * held[n] + value for n in range(modes)]
            local[at, :] = tree_sum([weight_of[n] * held[n] for n in range(modes)])
            return held

        lax.fori_loop(
            0, length, convolve, [jnp.zeros((ROWS, LANES), jnp.float32)] * modes, unroll=4
        )

    def out_copy(half):
        part = pl.ds(half * ROWS * LANES, ROWS * LANES)
        return pltpu.make_async_copy(staged.at[part], out.at[part], out_sem.at[half])

    @pl.when(side == 1)
    def _():
        mate_copy(0).wait_recv()

    for half in range(half_count):
        first = half * mode_rows
        carry[...] = jnp.zeros(carry.shape, jnp.float32)

        def take_state(sender, _, half=half, first=first):
            pltpu.make_async_remote_copy(
                src_ref=pair_state,
                dst_ref=states.at[sender, half],
                send_sem=state_send.at[sender, half],
                recv_sem=state_recv.at[sender, half],
                device_id={"seq": 2 * sender + half},
                device_id_type=MESH,
            ).wait_recv()
            carry[...] = carry[...] * pair_decay[first : first + mode_rows, :] + states[
                sender, half
            ].astype(jnp.float32)
            return 0

        lax.fori_loop(0, pair, take_state, 0)

        @pl.when(side == 1)
        def _(half=half, first=first):
            carry[...] = carry[...] * block_decay[first : first + mode_rows, :] + mate_state[
                half
            ].astype(jnp.float32)

        carry[...] = carry[...] * weights[first : first + mode_rows, :]
        rate_of = of_modes(decay, half)
        skip_here = skip[half * ROWS : (half + 1) * ROWS, :]

        def finish(t, held, half=half, rate_of=rate_of, skip_here=skip_here):
            at = rows_of(half * half_rows + t * ROWS)
            held = [rate_of[n] * held[n] for n in range(modes)]
            long_part = (local[at, :] + tree_sum(held)).astype(jnp.bfloat16).astype(jnp.float32)
            local[at, :] = mixed_q[at, :] * (long_part + skip_here * product[at, :])
            return held

        lax.fori_loop(0, length, finish, of_modes(carry, 0), unroll=4)
        for row in range(ROWS):
            gated = local[pl.ds(half * half_rows + row, length, stride=ROWS), :].astype(jnp.bfloat16)
            first_channel = (half * ROWS + row) * LANES
            staged[first_channel : first_channel + LANES, :] = lax.dot_general(
                eye, gated, across, preferred_element_type=jnp.float32
            ).astype(jnp.bfloat16)

        out_copy(half).start()

    for half in range(half_count):
        out_copy(half).wait()

    def drain_params(step, _):
        for kind in range(2):
            param_copy(kind, step).wait_send()
        return 0

    lax.fori_loop(1, seq_count, drain_params, 0)

    @pl.when(me < seq_count - 1)
    def _():
        halo_copy.wait_send()

    mate_copy(1 - side).wait_send()

    @pl.when(side == 0)
    def _():
        mate_copy(0).wait_send()

    for_later(lambda copy: copy.wait_send())


def tree_sum(terms):
    while len(terms) > 1:
        terms = [terms[i] + terms[i + 1] for i in range(0, len(terms), 2)]
    return terms[0]


def body(projected, short_taps, skip_gain, residue, decay_rate):
    seq_count = lax.axis_size("seq")
    _, width, length = projected.shape
    filters, modes = residue.shape
    block_count = width // LANES
    half_count = block_count // ROWS
    assert half_count == 2 and seq_count % 2 == 0
    call = functools.partial(kernel, seq_count, modes, half_count, length, filters)
    hbm = pl.BlockSpec(memory_space=pltpu.HBM)
    mode_rows = modes * ROWS
    f32, bf16 = jnp.float32, jnp.bfloat16
    dma = pltpu.SemaphoreType.DMA
    return pl.pallas_call(
        call,
        out_shape=jax.ShapeDtypeStruct((width, length), bf16),
        in_specs=[hbm] * 5,
        out_specs=hbm,
        scratch_shapes=[
            pltpu.VMEM((modes, filters), f32),
            pltpu.VMEM((modes, filters), f32),
            pltpu.VMEM((3, width, length), bf16),
            pltpu.VMEM((3, 3, width), f32),
            pltpu.VMEM((block_count, LANES), f32),
            pltpu.VMEM((9, block_count, LANES), f32),
            pltpu.VMEM((3 * length * block_count, LANES), f32),
            pltpu.VMEM((length * block_count, LANES), f32),
            pltpu.VMEM((length * block_count, LANES), f32),
            pltpu.VMEM((length * block_count, LANES), f32),
            pltpu.VMEM((2, modes, filters), f32),
            pltpu.VMEM((seq_count, 2, modes, filters), f32),
            pltpu.VMEM((half_count * mode_rows, LANES), f32),
            pltpu.VMEM((half_count * mode_rows, LANES), f32),
            pltpu.VMEM((half_count * mode_rows, LANES), f32),
            pltpu.VMEM((half_count * mode_rows, LANES), f32),
            pltpu.VMEM((half_count * mode_rows, LANES), f32),
            pltpu.VMEM((6, block_count, LANES), bf16),
            pltpu.VMEM((6, block_count, LANES), bf16),
            pltpu.VMEM((half_count, mode_rows, LANES), bf16),
            pltpu.VMEM((half_count, mode_rows, LANES), bf16),
            pltpu.VMEM((mode_rows, LANES), bf16),
            pltpu.VMEM((seq_count // 2, half_count, mode_rows, LANES), bf16),
            pltpu.VMEM((mode_rows, LANES), f32),
            pltpu.VMEM((width, length), bf16),
            dma((3,)),
            dma((2,)),
            dma((4,)),
            dma((2, seq_count)),
            dma((2, seq_count)),
            dma,
            dma,
            dma((2,)),
            dma((2,)),
            dma((seq_count // 2, 2)),
            dma((seq_count // 2, 2)),
        ],
        compiler_params=pltpu.CompilerParams(
            collective_id=0, has_side_effects=True, vmem_limit_bytes=60 * 1024 * 1024
        ),
    )(
        projected,
        short_taps,
        skip_gain.reshape(skip_gain.shape[0] // LANES, LANES),
        residue.T,
        decay_rate.T,
    )


def solution(mesh):
    in_specs = (P(None, "mp", "seq"), P(), P(), P("seq", None), P("seq", None))
    out_specs = P("mp", "seq")
    return jax.shard_map(body, mesh=mesh, in_specs=in_specs, out_specs=out_specs, check_vma=False)
```

```python
import functools

import jax
import jax.numpy as jnp
from jax import lax
from jax.experimental import pallas as pl
from jax.experimental.pallas import tpu as pltpu
from jax.sharding import PartitionSpec as P

MESH = pl.DeviceIdType.MESH
LANES = 128
ROWS = 8


def rows_of(first, count=ROWS):
    return pl.ds(pl.multiple_of(first, ROWS), count)


def kernel(
    seq_count,
    modes,
    half_count,
    length,
    filters,
    projected,
    taps_hbm,
    skip_hbm,
    residue_hbm,
    rate_hbm,
    out,
    residue,
    rate,
    streams,
    taps_raw,
    skip,
    taps,
    laid,
    product,
    mixed_q,
    local,
    own_params,
    params,
    rates,
    weights,
    decay,
    block_decay,
    pair_decay,
    halo_out,
    halo_in,
    own_state,
    mate_state,
    pair_state,
    states,
    carry,
    in_sem,
    tap_sem,
    param_send,
    param_recv,
    halo_send,
    halo_recv,
    mate_send,
    mate_recv,
    state_send,
    state_recv,
):
    me = lax.axis_index("seq")
    group = lax.axis_index("mp")
    block_count = half_count * ROWS
    width = block_count * LANES
    half_rows = length * ROWS
    mode_rows = modes * ROWS
    side = lax.rem(me, 2)
    pair = lax.div(me, 2)
    pair_count = seq_count // 2
    mate = me + 1 - 2 * side

    in_copies = [
        pltpu.make_async_copy(projected.at[s], streams.at[s], in_sem.at[s]) for s in range(3)
    ]
    tap_copy = pltpu.make_async_copy(
        taps_hbm.at[:, :, pl.ds(pl.multiple_of(group * width, LANES), width)],
        taps_raw,
        tap_sem.at[0],
    )
    skip_copy = pltpu.make_async_copy(
        skip_hbm.at[rows_of(group * block_count, block_count)], skip, tap_sem.at[1]
    )
    rate_copy = pltpu.make_async_copy(rate_hbm, rate, tap_sem.at[2])
    residue_copy = pltpu.make_async_copy(residue_hbm, residue, tap_sem.at[3])
    rate_copy.start()
    residue_copy.start()
    for copy in in_copies:
        copy.start()
    tap_copy.start()
    skip_copy.start()

    barrier = pltpu.get_barrier_semaphore()

    def greet(step, _):
        peer = lax.rem(me + step, seq_count)
        pl.semaphore_signal(barrier, inc=1, device_id={"seq": peer}, device_id_type=MESH)
        return 0

    lax.fori_loop(1, seq_count, greet, 0)
    rate_copy.wait()
    residue_copy.wait()
    own_params[0] = rate[...]
    own_params[1] = residue[...] * jnp.sqrt(rate[...])
    params[me] = own_params[...]
    pl.semaphore_wait(barrier, seq_count - 1)

    def param_copy(kind, step):
        peer = lax.rem(me + step, seq_count)
        return pltpu.make_async_remote_copy(
            src_ref=own_params.at[kind],
            dst_ref=params.at[me, kind],
            send_sem=param_send.at[kind, step],
            recv_sem=param_recv.at[kind, step],
            device_id={"seq": peer},
            device_id_type=MESH,
        )

    def send_params(kind):
        def send(step, _):
            param_copy(kind, step).start()
            return 0

        lax.fori_loop(1, seq_count, send, 0)

    send_params(0)

    for s in range(3):
        in_copies[s].wait()
        for block in range(block_count):
            half, row = divmod(block, ROWS)
            laid[pl.ds((s * half_count + half) * half_rows + row, length, stride=ROWS), :] = (
                streams[s, block * LANES : (block + 1) * LANES, :].T.astype(jnp.float32)
            )

    def laid_row(s, half, t):
        return laid[rows_of((s * half_count + half) * half_rows + t * ROWS), :]

    for s in range(3):
        for back in range(2):
            pieces = [laid_row(s, half, length - 2 + back) for half in range(half_count)]
            halo_out[s * 2 + back] = jnp.concatenate(pieces, axis=0).astype(jnp.bfloat16)

    halo_copy = pltpu.make_async_remote_copy(
        src_ref=halo_out,
        dst_ref=halo_in,
        send_sem=halo_send,
        recv_sem=halo_recv,
        device_id={"seq": lax.rem(me + 1, seq_count)},
        device_id_type=MESH,
    )

    @pl.when(me < seq_count - 1)
    def _():
        halo_copy.start()

    send_params(1)
    tap_copy.wait()
    skip_copy.wait()
    for lag in range(3):
        for s in range(3):
            for block in range(block_count):
                taps[lag * 3 + s, block : block + 1, :] = taps_raw[
                    lag, s : s + 1, block * LANES : (block + 1) * LANES
                ]

    def tap_rows(half):
        return [
            [taps[lag * 3 + s, half * ROWS : (half + 1) * ROWS, :] for lag in range(3)]
            for s in range(3)
        ]

    def put_mixed(half, t, now, before, earlier, tap):
        q, k, v = [
            tap[s][0] * now[s] + tap[s][1] * before[s] + tap[s][2] * earlier[s] for s in range(3)
        ]
        at = rows_of(half * half_rows + t * ROWS)
        mixed_q[at, :] = q
        product[at, :] = (k * v).astype(jnp.bfloat16).astype(jnp.float32)

    for half in range(half_count):
        tap = tap_rows(half)

        def mix(t, past, half=half, tap=tap):
            before, earlier = past
            now = [laid_row(s, half, t) for s in range(3)]
            put_mixed(half, t, now, before, earlier, tap)
            return now, before

        first = [[laid_row(s, half, t) for s in range(3)] for t in range(2)]
        lax.fori_loop(2, length, mix, (first[1], first[0]), unroll=6)

    @pl.when(me > 0)
    def _():
        halo_copy.wait_recv()

    @pl.when(me == 0)
    def _():
        halo_in[...] = jnp.zeros(halo_in.shape, halo_in.dtype)

    for half in range(half_count):
        tap = tap_rows(half)
        past = [
            [
                halo_in[s * 2 + back].astype(jnp.float32)[half * ROWS : (half + 1) * ROWS]
                for s in range(3)
            ]
            for back in range(2)
        ]
        first = [[laid_row(s, half, t) for s in range(3)] for t in range(2)]
        put_mixed(half, 0, first[0], past[1], past[0], tap)
        put_mixed(half, 1, first[1], first[0], past[1], tap)

    def take_params(kind, target):
        def take(step, _):
            param_copy(kind, step).wait_recv()
            return 0

        lax.fori_loop(1, seq_count, take, 0)
        for block in range(block_count):
            half, row = divmod(block, ROWS)
            if filters >= LANES:
                per = filters // LANES
                lane = (block % per) * LANES
                piece = params[block // per, kind, :, lane : lane + LANES]
            else:
                per = LANES // filters
                piece = jnp.concatenate(
                    [params[block * per + part, kind] for part in range(per)], axis=1
                )
            target[pl.ds(half * mode_rows + row, modes, stride=ROWS), :] = piece

    take_params(0, rates)
    decay[...] = jnp.exp(-rates[...])

    def of_modes(ref, half):
        first = half * mode_rows
        return [ref[rows_of(first + n * ROWS), :] for n in range(modes)]

    def find_state(half):
        rate_of = of_modes(decay, half)

        def gather_state(t, held):
            value = product[rows_of(half * half_rows + t * ROWS), :]
            return [rate_of[n] * held[n] + value for n in range(modes)]

        held = lax.fori_loop(
            0,
            length,
            gather_state,
            [jnp.zeros((ROWS, LANES), jnp.float32)] * modes,
            unroll=8,
        )
        own_state[half] = jnp.concatenate(held, axis=0).astype(jnp.bfloat16)

    def mate_copy(half):
        return pltpu.make_async_remote_copy(
            src_ref=own_state.at[half],
            dst_ref=mate_state.at[half],
            send_sem=mate_send.at[half],
            recv_sem=mate_recv.at[half],
            device_id={"seq": mate},
            device_id_type=MESH,
        )

    find_state(1 - side)
    mate_copy(1 - side).start()
    block_decay[...] = jnp.exp(-float(length) * rates[...])
    pair_decay[...] = block_decay[...] * block_decay[...]
    find_state(side)

    @pl.when(side == 0)
    def _():
        mate_copy(0).start()

    def state_copy(later, target_side):
        return pltpu.make_async_remote_copy(
            src_ref=pair_state,
            dst_ref=states.at[pair, side],
            send_sem=state_send.at[later, target_side],
            recv_sem=state_recv.at[pair, side],
            device_id={"seq": 2 * later + target_side},
            device_id_type=MESH,
        )

    def for_later(action):
        def step(later, _):
            for target_side in range(2):
                action(state_copy(later, target_side))
            return 0

        lax.fori_loop(pair + 1, pair_count, step, 0)

    mate_copy(side).wait_recv()
    own_part = own_state[side].astype(jnp.float32)
    mate_part = mate_state[side].astype(jnp.float32)
    scale = block_decay[rows_of(side * mode_rows, mode_rows), :]
    even = jnp.where(side == 0, own_part, mate_part)
    odd = jnp.where(side == 0, mate_part, own_part)
    pair_state[...] = (scale * even + odd).astype(jnp.bfloat16)
    for_later(lambda copy: copy.start())
    take_params(1, weights)

    for half in range(half_count):
        rate_of = of_modes(decay, half)
        weight_of = of_modes(weights, half)

        def convolve(t, held, half=half, rate_of=rate_of, weight_of=weight_of):
            at = rows_of(half * half_rows + t * ROWS)
            value = product[at, :]
            held = [rate_of[n] * held[n] + value for n in range(modes)]
            local[at, :] = tree_sum([weight_of[n] * held[n] for n in range(modes)])
            return held

        lax.fori_loop(
            0, length, convolve, [jnp.zeros((ROWS, LANES), jnp.float32)] * modes, unroll=4
        )

    @pl.when(side == 1)
    def _():
        mate_copy(0).wait_recv()

    for half in range(half_count):
        first = half * mode_rows
        carry[...] = jnp.zeros(carry.shape, jnp.float32)

        def take_state(sender, _, half=half, first=first):
            pltpu.make_async_remote_copy(
                src_ref=pair_state,
                dst_ref=states.at[sender, half],
                send_sem=state_send.at[sender, half],
                recv_sem=state_recv.at[sender, half],
                device_id={"seq": 2 * sender + half},
                device_id_type=MESH,
            ).wait_recv()
            carry[...] = carry[...] * pair_decay[first : first + mode_rows, :] + states[
                sender, half
            ].astype(jnp.float32)
            return 0

        lax.fori_loop(0, pair, take_state, 0)

        @pl.when(side == 1)
        def _(half=half, first=first):
            carry[...] = carry[...] * block_decay[first : first + mode_rows, :] + mate_state[
                half
            ].astype(jnp.float32)

        carry[...] = carry[...] * weights[first : first + mode_rows, :]
        rate_of = of_modes(decay, half)
        skip_here = skip[half * ROWS : (half + 1) * ROWS, :]

        def finish(t, held, half=half, rate_of=rate_of, skip_here=skip_here):
            at = rows_of(half * half_rows + t * ROWS)
            held = [rate_of[n] * held[n] for n in range(modes)]
            long_part = (local[at, :] + tree_sum(held)).astype(jnp.bfloat16).astype(jnp.float32)
            local[at, :] = mixed_q[at, :] * (long_part + skip_here * product[at, :])
            return held

        lax.fori_loop(0, length, finish, of_modes(carry, 0), unroll=4)
        for row in range(ROWS):
            gated = local[pl.ds(half * half_rows + row, length, stride=ROWS), :].astype(jnp.bfloat16)
            first_channel = (half * ROWS + row) * LANES
            out[first_channel : first_channel + LANES, :] = gated.T


    def drain_params(step, _):
        for kind in range(2):
            param_copy(kind, step).wait_send()
        return 0

    lax.fori_loop(1, seq_count, drain_params, 0)

    @pl.when(me < seq_count - 1)
    def _():
        halo_copy.wait_send()

    mate_copy(1 - side).wait_send()

    @pl.when(side == 0)
    def _():
        mate_copy(0).wait_send()

    for_later(lambda copy: copy.wait_send())


def tree_sum(terms):
    while len(terms) > 1:
        terms = [terms[i] + terms[i + 1] for i in range(0, len(terms), 2)]
    return terms[0]


def body(projected, short_taps, skip_gain, residue, decay_rate):
    seq_count = lax.axis_size("seq")
    _, width, length = projected.shape
    filters, modes = residue.shape
    block_count = width // LANES
    half_count = block_count // ROWS
    assert half_count == 2 and seq_count % 2 == 0
    call = functools.partial(kernel, seq_count, modes, half_count, length, filters)
    hbm = pl.BlockSpec(memory_space=pltpu.HBM)
    mode_rows = modes * ROWS
    f32, bf16 = jnp.float32, jnp.bfloat16
    dma = pltpu.SemaphoreType.DMA
    return pl.pallas_call(
        call,
        out_shape=pltpu.VMEM((width, length), bf16),
        in_specs=[hbm] * 5,
        out_specs=pl.BlockSpec(memory_space=pltpu.VMEM),
        scratch_shapes=[
            pltpu.VMEM((modes, filters), f32),
            pltpu.VMEM((modes, filters), f32),
            pltpu.VMEM((3, width, length), bf16),
            pltpu.VMEM((3, 3, width), f32),
            pltpu.VMEM((block_count, LANES), f32),
            pltpu.VMEM((9, block_count, LANES), f32),
            pltpu.VMEM((3 * length * block_count, LANES), f32),
            pltpu.VMEM((length * block_count, LANES), f32),
            pltpu.VMEM((length * block_count, LANES), f32),
            pltpu.VMEM((length * block_count, LANES), f32),
            pltpu.VMEM((2, modes, filters), f32),
            pltpu.VMEM((seq_count, 2, modes, filters), f32),
            pltpu.VMEM((half_count * mode_rows, LANES), f32),
            pltpu.VMEM((half_count * mode_rows, LANES), f32),
            pltpu.VMEM((half_count * mode_rows, LANES), f32),
            pltpu.VMEM((half_count * mode_rows, LANES), f32),
            pltpu.VMEM((half_count * mode_rows, LANES), f32),
            pltpu.VMEM((6, block_count, LANES), bf16),
            pltpu.VMEM((6, block_count, LANES), bf16),
            pltpu.VMEM((half_count, mode_rows, LANES), bf16),
            pltpu.VMEM((half_count, mode_rows, LANES), bf16),
            pltpu.VMEM((mode_rows, LANES), bf16),
            pltpu.VMEM((seq_count // 2, half_count, mode_rows, LANES), bf16),
            pltpu.VMEM((mode_rows, LANES), f32),
            dma((3,)),
            dma((4,)),
            dma((2, seq_count)),
            dma((2, seq_count)),
            dma,
            dma,
            dma((2,)),
            dma((2,)),
            dma((seq_count // 2, 2)),
            dma((seq_count // 2, 2)),
        ],
        compiler_params=pltpu.CompilerParams(
            collective_id=0, has_side_effects=True, vmem_limit_bytes=60 * 1024 * 1024
        ),
    )(
        projected,
        short_taps,
        skip_gain.reshape(skip_gain.shape[0] // LANES, LANES),
        residue.T,
        decay_rate.T,
    )


def solution(mesh):
    in_specs = (P(None, "mp", "seq"), P(), P(), P("seq", None), P("seq", None))
    out_specs = P("mp", "seq")
    return jax.shard_map(body, mesh=mesh, in_specs=in_specs, out_specs=out_specs, check_vma=False)
```

```python
import functools

import jax
import jax.numpy as jnp
from jax import lax
from jax.experimental import pallas as pl
from jax.experimental.pallas import tpu as pltpu
from jax.sharding import PartitionSpec as P

MESH = pl.DeviceIdType.MESH
LANES = 128
ROWS = 8


def rows_of(first, count=ROWS):
    return pl.ds(pl.multiple_of(first, ROWS), count)


def kernel(
    seq_count,
    modes,
    half_count,
    length,
    filters,
    projected,
    taps_hbm,
    skip_hbm,
    residue_hbm,
    rate_hbm,
    out,
    residue,
    rate,
    streams,
    taps_raw,
    skip,
    taps,
    laid,
    product,
    mixed_q,
    local,
    own_params,
    params,
    rates,
    weights,
    decay,
    block_decay,
    pair_decay,
    halo_out,
    halo_in,
    own_state,
    mate_state,
    pair_state,
    states,
    carry,
    prefix,
    mate_prefix,
    in_sem,
    tap_sem,
    param_send,
    param_recv,
    halo_send,
    halo_recv,
    mate_send,
    mate_recv,
    state_send,
    state_recv,
    prefix_send,
    prefix_recv,
):
    me = lax.axis_index("seq")
    group = lax.axis_index("mp")
    block_count = half_count * ROWS
    width = block_count * LANES
    half_rows = length * ROWS
    mode_rows = modes * ROWS
    side = lax.rem(me, 2)
    pair = lax.div(me, 2)
    pair_count = seq_count // 2
    mate = me + 1 - 2 * side

    in_copies = [
        pltpu.make_async_copy(projected.at[s], streams.at[s], in_sem.at[s]) for s in range(3)
    ]
    tap_copy = pltpu.make_async_copy(
        taps_hbm.at[:, :, pl.ds(pl.multiple_of(group * width, LANES), width)],
        taps_raw,
        tap_sem.at[0],
    )
    skip_copy = pltpu.make_async_copy(
        skip_hbm.at[rows_of(group * block_count, block_count)], skip, tap_sem.at[1]
    )
    rate_copy = pltpu.make_async_copy(rate_hbm, rate, tap_sem.at[2])
    residue_copy = pltpu.make_async_copy(residue_hbm, residue, tap_sem.at[3])
    rate_copy.start()
    residue_copy.start()
    for s in (1, 2, 0):
        in_copies[s].start()
    tap_copy.start()
    skip_copy.start()

    def turn(s):
        in_copies[s].wait()
        for block in range(block_count):
            half, row = divmod(block, ROWS)
            laid[pl.ds((s * half_count + half) * half_rows + row, length, stride=ROWS), :] = (
                streams[s, block * LANES : (block + 1) * LANES, :].T.astype(jnp.float32)
            )

    barrier = pltpu.get_barrier_semaphore()

    def greet(step, _):
        peer = lax.rem(me + step, seq_count)
        pl.semaphore_signal(barrier, inc=1, device_id={"seq": peer}, device_id_type=MESH)
        return 0

    lax.fori_loop(1, seq_count, greet, 0)
    rate_copy.wait()
    residue_copy.wait()
    own_params[0] = rate[...]
    own_params[1] = residue[...] * jnp.sqrt(rate[...])
    params[me] = own_params[...]
    turn(1)
    pl.semaphore_wait(barrier, seq_count - 1)

    def param_copy(kind, step):
        peer = lax.rem(me + step, seq_count)
        return pltpu.make_async_remote_copy(
            src_ref=own_params.at[kind],
            dst_ref=params.at[me, kind],
            send_sem=param_send.at[kind, step],
            recv_sem=param_recv.at[kind, step],
            device_id={"seq": peer},
            device_id_type=MESH,
        )

    def send_params(kind):
        def send(step, _):
            param_copy(kind, step).start()
            return 0

        lax.fori_loop(1, seq_count, send, 0)

    send_params(0)

    def laid_row(s, half, t):
        return laid[rows_of((s * half_count + half) * half_rows + t * ROWS), :]

    turn(2)

    def halo_copy(s):
        return pltpu.make_async_remote_copy(
            src_ref=halo_out.at[s],
            dst_ref=halo_in.at[s],
            send_sem=halo_send.at[s],
            recv_sem=halo_recv.at[s],
            device_id={"seq": lax.rem(me + 1, seq_count)},
            device_id_type=MESH,
        )

    def send_halo(s):
        for back in range(2):
            pieces = [laid_row(s, half, length - 2 + back) for half in range(half_count)]
            halo_out[s, back] = jnp.concatenate(pieces, axis=0).astype(jnp.bfloat16)

        @pl.when(me < seq_count - 1)
        def _():
            halo_copy(s).start()

    def take_halo(s):
        @pl.when(me > 0)
        def _():
            halo_copy(s).wait_recv()

        @pl.when(me == 0)
        def _():
            halo_in[s] = jnp.zeros(halo_in.shape[1:], halo_in.dtype)

    send_halo(1)
    send_halo(2)
    send_params(1)
    tap_copy.wait()
    skip_copy.wait()
    for lag in range(3):
        for s in range(3):
            for block in range(block_count):
                taps[lag * 3 + s, block : block + 1, :] = taps_raw[
                    lag, s : s + 1, block * LANES : (block + 1) * LANES
                ]

    def mix_streams(which, put):
        taps_of = [
            [
                [taps[lag * 3 + s, half * ROWS : (half + 1) * ROWS, :] for lag in range(3)]
                for s in which
            ]
            for half in range(half_count)
        ]

        def mix_at(half, t, now, before, earlier):
            put(
                rows_of(half * half_rows + t * ROWS),
                [
                    tap[0] * now[i] + tap[1] * before[i] + tap[2] * earlier[i]
                    for i, tap in enumerate(taps_of[half])
                ],
            )

        for half in range(half_count):

            def mix(t, past, half=half):
                before, earlier = past
                now = [laid_row(s, half, t) for s in which]
                mix_at(half, t, now, before, earlier)
                return now, before

            first = [[laid_row(s, half, t) for s in which] for t in range(2)]
            lax.fori_loop(2, length, mix, (first[1], first[0]), unroll=6)

        for s in which:
            take_halo(s)
        for half in range(half_count):
            past = [
                [
                    halo_in[s, back].astype(jnp.float32)[half * ROWS : (half + 1) * ROWS]
                    for s in which
                ]
                for back in range(2)
            ]
            first = [[laid_row(s, half, t) for s in which] for t in range(2)]
            mix_at(half, 0, first[0], past[1], past[0])
            mix_at(half, 1, first[1], first[0], past[1])

    def put_product(at, mixed):
        product[at, :] = (mixed[0] * mixed[1]).astype(jnp.bfloat16).astype(jnp.float32)

    def put_q(at, mixed):
        mixed_q[at, :] = mixed[0]

    mix_streams((1, 2), put_product)

    def take_params(kind, target):
        def take(step, _):
            param_copy(kind, step).wait_recv()
            return 0

        lax.fori_loop(1, seq_count, take, 0)
        for block in range(block_count):
            half, row = divmod(block, ROWS)
            if filters >= LANES:
                per = filters // LANES
                lane = (block % per) * LANES
                piece = params[block // per, kind, :, lane : lane + LANES]
            else:
                per = LANES // filters
                piece = jnp.concatenate(
                    [params[block * per + part, kind] for part in range(per)], axis=1
                )
            target[pl.ds(half * mode_rows + row, modes, stride=ROWS), :] = piece

    take_params(0, rates)
    decay[...] = jnp.exp(-rates[...])

    def of_modes(ref, half):
        first = half * mode_rows
        return [ref[rows_of(first + n * ROWS), :] for n in range(modes)]

    def find_state(half):
        rate_of = of_modes(decay, half)

        def gather_state(t, held):
            value = product[rows_of(half * half_rows + t * ROWS), :]
            return [rate_of[n] * held[n] + value for n in range(modes)]

        held = lax.fori_loop(
            0,
            length,
            gather_state,
            [jnp.zeros((ROWS, LANES), jnp.float32)] * modes,
            unroll=8,
        )
        own_state[half] = jnp.concatenate(held, axis=0).astype(jnp.bfloat16)

    def mate_copy(half):
        return pltpu.make_async_remote_copy(
            src_ref=own_state.at[half],
            dst_ref=mate_state.at[half],
            send_sem=mate_send.at[half],
            recv_sem=mate_recv.at[half],
            device_id={"seq": mate},
            device_id_type=MESH,
        )

    find_state(1 - side)
    mate_copy(1 - side).start()
    block_decay[...] = jnp.exp(-float(length) * rates[...])
    pair_decay[...] = block_decay[...] * block_decay[...]
    find_state(side)

    @pl.when(side == 0)
    def _():
        mate_copy(0).start()

    def state_copy(sender, later):
        return pltpu.make_async_remote_copy(
            src_ref=pair_state,
            dst_ref=states.at[sender],
            send_sem=state_send.at[later],
            recv_sem=state_recv.at[sender],
            device_id={"seq": 2 * later + side},
            device_id_type=MESH,
        )

    def for_later(action):
        def step(later, _):
            action(state_copy(pair, later))
            return 0

        lax.fori_loop(pair + 1, pair_count, step, 0)

    mate_copy(side).wait_recv()
    own_part = own_state[side].astype(jnp.float32)
    mate_part = mate_state[side].astype(jnp.float32)
    scale = block_decay[rows_of(side * mode_rows, mode_rows), :]
    even = jnp.where(side == 0, own_part, mate_part)
    odd = jnp.where(side == 0, mate_part, own_part)
    pair_state[...] = (scale * even + odd).astype(jnp.bfloat16)
    for_later(lambda copy: copy.start())
    turn(0)
    send_halo(0)
    take_params(1, weights)

    for half in range(half_count):
        rate_of = of_modes(decay, half)
        weight_of = of_modes(weights, half)

        def convolve(t, held, half=half, rate_of=rate_of, weight_of=weight_of):
            at = rows_of(half * half_rows + t * ROWS)
            value = product[at, :]
            held = [rate_of[n] * held[n] + value for n in range(modes)]
            local[at, :] = tree_sum([weight_of[n] * held[n] for n in range(modes)])
            return held

        lax.fori_loop(
            0, length, convolve, [jnp.zeros((ROWS, LANES), jnp.float32)] * modes, unroll=4
        )

    prefix_copy = pltpu.make_async_remote_copy(
        src_ref=prefix,
        dst_ref=mate_prefix,
        send_sem=prefix_send,
        recv_sem=prefix_recv,
        device_id={"seq": mate},
        device_id_type=MESH,
    )
    prefix[...] = jnp.zeros(prefix.shape, jnp.float32)

    def take_state(sender, _):
        state_copy(sender, sender).wait_recv()
        prefix[...] = prefix[...] * pair_decay[rows_of(side * mode_rows, mode_rows), :] + states[
            sender
        ].astype(jnp.float32)
        return 0

    lax.fori_loop(0, pair, take_state, 0)

    @pl.when(pair > 0)
    def _():
        prefix_copy.start()

    mix_streams((0,), put_q)

    @pl.when(side == 1)
    def _():
        mate_copy(0).wait_recv()

    for turn_at in range(2):
        half = side if turn_at == 0 else 1 - side
        here = rows_of(half * mode_rows, mode_rows)
        if turn_at == 0:
            carry[...] = prefix[...]
        else:

            @pl.when(pair > 0)
            def _():
                prefix_copy.wait_recv()
                carry[...] = mate_prefix[...]

            @pl.when(pair == 0)
            def _():
                carry[...] = jnp.zeros(carry.shape, jnp.float32)

        @pl.when(side == 1)
        def _(half=half, here=here):
            carry[...] = carry[...] * block_decay[here, :] + mate_state[half].astype(jnp.float32)

        carry[...] = carry[...] * weights[here, :]
        rate_of = of_modes(decay, half)
        skip_here = skip[rows_of(half * ROWS), :]

        def finish(t, held, half=half, rate_of=rate_of, skip_here=skip_here):
            at = rows_of(half * half_rows + t * ROWS)
            held = [rate_of[n] * held[n] for n in range(modes)]
            long_part = (local[at, :] + tree_sum(held)).astype(jnp.bfloat16).astype(jnp.float32)
            local[at, :] = mixed_q[at, :] * (long_part + skip_here * product[at, :])
            return held

        lax.fori_loop(0, length, finish, of_modes(carry, 0), unroll=4)
        for row in range(ROWS):
            gated = local[pl.ds(half * half_rows + row, length, stride=ROWS), :].astype(jnp.bfloat16)
            first_channel = pl.multiple_of((half * ROWS + row) * LANES, LANES)
            out[pl.ds(first_channel, LANES), :] = gated.T


    def drain_params(step, _):
        for kind in range(2):
            param_copy(kind, step).wait_send()
        return 0

    lax.fori_loop(1, seq_count, drain_params, 0)

    @pl.when(me < seq_count - 1)
    def _():
        for s in range(3):
            halo_copy(s).wait_send()

    mate_copy(1 - side).wait_send()

    @pl.when(side == 0)
    def _():
        mate_copy(0).wait_send()

    for_later(lambda copy: copy.wait_send())

    @pl.when(pair > 0)
    def _():
        prefix_copy.wait_send()


def tree_sum(terms):
    while len(terms) > 1:
        terms = [terms[i] + terms[i + 1] for i in range(0, len(terms), 2)]
    return terms[0]


def body(projected, short_taps, skip_gain, residue, decay_rate):
    seq_count = lax.axis_size("seq")
    _, width, length = projected.shape
    filters, modes = residue.shape
    block_count = width // LANES
    half_count = block_count // ROWS
    assert half_count == 2 and seq_count % 2 == 0
    call = functools.partial(kernel, seq_count, modes, half_count, length, filters)
    hbm = pl.BlockSpec(memory_space=pltpu.HBM)
    mode_rows = modes * ROWS
    f32, bf16 = jnp.float32, jnp.bfloat16
    dma = pltpu.SemaphoreType.DMA
    return pl.pallas_call(
        call,
        out_shape=pltpu.VMEM((width, length), bf16),
        in_specs=[hbm] * 5,
        out_specs=pl.BlockSpec(memory_space=pltpu.VMEM),
        scratch_shapes=[
            pltpu.VMEM((modes, filters), f32),
            pltpu.VMEM((modes, filters), f32),
            pltpu.VMEM((3, width, length), bf16),
            pltpu.VMEM((3, 3, width), f32),
            pltpu.VMEM((block_count, LANES), f32),
            pltpu.VMEM((9, block_count, LANES), f32),
            pltpu.VMEM((3 * length * block_count, LANES), f32),
            pltpu.VMEM((length * block_count, LANES), f32),
            pltpu.VMEM((length * block_count, LANES), f32),
            pltpu.VMEM((length * block_count, LANES), f32),
            pltpu.VMEM((2, modes, filters), f32),
            pltpu.VMEM((seq_count, 2, modes, filters), f32),
            pltpu.VMEM((half_count * mode_rows, LANES), f32),
            pltpu.VMEM((half_count * mode_rows, LANES), f32),
            pltpu.VMEM((half_count * mode_rows, LANES), f32),
            pltpu.VMEM((half_count * mode_rows, LANES), f32),
            pltpu.VMEM((half_count * mode_rows, LANES), f32),
            pltpu.VMEM((3, 2, block_count, LANES), bf16),
            pltpu.VMEM((3, 2, block_count, LANES), bf16),
            pltpu.VMEM((half_count, mode_rows, LANES), bf16),
            pltpu.VMEM((half_count, mode_rows, LANES), bf16),
            pltpu.VMEM((mode_rows, LANES), bf16),
            pltpu.VMEM((seq_count // 2, mode_rows, LANES), bf16),
            pltpu.VMEM((mode_rows, LANES), f32),
            pltpu.VMEM((mode_rows, LANES), f32),
            pltpu.VMEM((mode_rows, LANES), f32),
            dma((3,)),
            dma((4,)),
            dma((2, seq_count)),
            dma((2, seq_count)),
            dma((3,)),
            dma((3,)),
            dma((2,)),
            dma((2,)),
            dma((seq_count // 2,)),
            dma((seq_count // 2,)),
            dma,
            dma,
        ],
        compiler_params=pltpu.CompilerParams(
            collective_id=0, has_side_effects=True, vmem_limit_bytes=60 * 1024 * 1024
        ),
    )(
        projected,
        short_taps,
        skip_gain.reshape(skip_gain.shape[0] // LANES, LANES),
        residue.T,
        decay_rate.T,
    )


def solution(mesh):
    in_specs = (P(None, "mp", "seq"), P(), P(), P("seq", None), P("seq", None))
    out_specs = P("mp", "seq")
    return jax.shard_map(body, mesh=mesh, in_specs=in_specs, out_specs=out_specs, check_vma=False)
```

```python
import functools

import jax
import jax.numpy as jnp
from jax import lax
from jax.experimental import pallas as pl
from jax.experimental.pallas import tpu as pltpu
from jax.sharding import PartitionSpec as P

MESH = pl.DeviceIdType.MESH
LANES = 128
ROWS = 8


def rows_of(first, count=ROWS):
    return pl.ds(pl.multiple_of(first, ROWS), count)


def kernel(
    seq_count,
    modes,
    half_count,
    length,
    filters,
    projected,
    taps_hbm,
    skip_hbm,
    residue_hbm,
    rate_hbm,
    out,
    residue,
    rate,
    streams,
    taps_raw,
    skip,
    taps,
    laid,
    product,
    mixed_q,
    local,
    own_params,
    params,
    rates,
    weights,
    decay,
    block_decay,
    pair_decay,
    halo_out,
    halo_in,
    own_state,
    mate_state,
    pair_state,
    states,
    carry,
    start,
    prefix,
    mate_prefix,
    in_sem,
    tap_sem,
    param_send,
    param_recv,
    halo_send,
    halo_recv,
    mate_send,
    mate_recv,
    state_send,
    state_recv,
    prefix_send,
    prefix_recv,
):
    me = lax.axis_index("seq")
    group = lax.axis_index("mp")
    block_count = half_count * ROWS
    width = block_count * LANES
    half_rows = length * ROWS
    mode_rows = modes * ROWS
    side = lax.rem(me, 2)
    pair = lax.div(me, 2)
    pair_count = seq_count // 2
    mate = me + 1 - 2 * side

    in_copies = [
        pltpu.make_async_copy(projected.at[s], streams.at[s], in_sem.at[s]) for s in range(3)
    ]
    tap_copy = pltpu.make_async_copy(
        taps_hbm.at[:, :, pl.ds(pl.multiple_of(group * width, LANES), width)],
        taps_raw,
        tap_sem.at[0],
    )
    skip_copy = pltpu.make_async_copy(
        skip_hbm.at[rows_of(group * block_count, block_count)], skip, tap_sem.at[1]
    )
    rate_copy = pltpu.make_async_copy(rate_hbm, rate, tap_sem.at[2])
    residue_copy = pltpu.make_async_copy(residue_hbm, residue, tap_sem.at[3])
    rate_copy.start()
    residue_copy.start()
    for s in (1, 2, 0):
        in_copies[s].start()
    tap_copy.start()
    skip_copy.start()

    def turn(s):
        in_copies[s].wait()
        for block in range(block_count):
            half, row = divmod(block, ROWS)
            laid[pl.ds((s * half_count + half) * half_rows + row, length, stride=ROWS), :] = (
                streams[s, block * LANES : (block + 1) * LANES, :].T.astype(jnp.float32)
            )

    barrier = pltpu.get_barrier_semaphore()

    def greet(step, _):
        peer = lax.rem(me + step, seq_count)
        pl.semaphore_signal(barrier, inc=1, device_id={"seq": peer}, device_id_type=MESH)
        return 0

    lax.fori_loop(1, seq_count, greet, 0)
    rate_copy.wait()
    residue_copy.wait()
    own_params[0] = rate[...]
    own_params[1] = residue[...] * jnp.sqrt(rate[...])
    params[me] = own_params[...]
    turn(1)
    pl.semaphore_wait(barrier, seq_count - 1)

    def param_copy(kind, step):
        peer = lax.rem(me + step, seq_count)
        return pltpu.make_async_remote_copy(
            src_ref=own_params.at[kind],
            dst_ref=params.at[me, kind],
            send_sem=param_send.at[kind, step],
            recv_sem=param_recv.at[kind, step],
            device_id={"seq": peer},
            device_id_type=MESH,
        )

    def send_params(kind):
        def send(step, _):
            param_copy(kind, step).start()
            return 0

        lax.fori_loop(1, seq_count, send, 0)

    send_params(0)

    def laid_row(s, half, t):
        return laid[rows_of((s * half_count + half) * half_rows + t * ROWS), :]

    turn(2)

    def halo_copy(s):
        return pltpu.make_async_remote_copy(
            src_ref=halo_out.at[s],
            dst_ref=halo_in.at[s],
            send_sem=halo_send.at[s],
            recv_sem=halo_recv.at[s],
            device_id={"seq": lax.rem(me + 1, seq_count)},
            device_id_type=MESH,
        )

    def send_halo(s):
        for back in range(2):
            pieces = [laid_row(s, half, length - 2 + back) for half in range(half_count)]
            halo_out[s, back] = jnp.concatenate(pieces, axis=0).astype(jnp.bfloat16)

        @pl.when(me < seq_count - 1)
        def _():
            halo_copy(s).start()

    def take_halo(s):
        @pl.when(me > 0)
        def _():
            halo_copy(s).wait_recv()

        @pl.when(me == 0)
        def _():
            halo_in[s] = jnp.zeros(halo_in.shape[1:], halo_in.dtype)

    send_halo(1)
    send_halo(2)
    turn(0)
    send_halo(0)
    send_params(1)
    tap_copy.wait()
    skip_copy.wait()
    for lag in range(3):
        for s in range(3):
            for block in range(block_count):
                taps[lag * 3 + s, block : block + 1, :] = taps_raw[
                    lag, s : s + 1, block * LANES : (block + 1) * LANES
                ]

    def mix_streams(which, put):
        taps_of = [
            [
                [taps[lag * 3 + s, half * ROWS : (half + 1) * ROWS, :] for lag in range(3)]
                for s in which
            ]
            for half in range(half_count)
        ]

        def mix_at(half, t, now, before, earlier):
            put(
                rows_of(half * half_rows + t * ROWS),
                [
                    tap[0] * now[i] + tap[1] * before[i] + tap[2] * earlier[i]
                    for i, tap in enumerate(taps_of[half])
                ],
            )

        for half in range(half_count):

            def mix(t, past, half=half):
                before, earlier = past
                now = [laid_row(s, half, t) for s in which]
                mix_at(half, t, now, before, earlier)
                return now, before

            first = [[laid_row(s, half, t) for s in which] for t in range(2)]
            lax.fori_loop(2, length, mix, (first[1], first[0]), unroll=6)

        for s in which:
            take_halo(s)
        for half in range(half_count):
            past = [
                [
                    halo_in[s, back].astype(jnp.float32)[half * ROWS : (half + 1) * ROWS]
                    for s in which
                ]
                for back in range(2)
            ]
            first = [[laid_row(s, half, t) for s in which] for t in range(2)]
            mix_at(half, 0, first[0], past[1], past[0])
            mix_at(half, 1, first[1], first[0], past[1])

    def put_product(at, mixed):
        product[at, :] = (mixed[0] * mixed[1]).astype(jnp.bfloat16).astype(jnp.float32)

    def put_q(at, mixed):
        mixed_q[at, :] = mixed[0]

    mix_streams((1, 2), put_product)

    def take_params(kind, target):
        def take(step, _):
            param_copy(kind, step).wait_recv()
            return 0

        lax.fori_loop(1, seq_count, take, 0)
        for block in range(block_count):
            half, row = divmod(block, ROWS)
            if filters >= LANES:
                per = filters // LANES
                lane = (block % per) * LANES
                piece = params[block // per, kind, :, lane : lane + LANES]
            else:
                per = LANES // filters
                piece = jnp.concatenate(
                    [params[block * per + part, kind] for part in range(per)], axis=1
                )
            target[pl.ds(half * mode_rows + row, modes, stride=ROWS), :] = piece

    take_params(0, rates)
    decay[...] = jnp.exp(-rates[...])

    def of_modes(ref, half):
        first = half * mode_rows
        return [ref[rows_of(first + n * ROWS), :] for n in range(modes)]

    def find_state(half):
        rate_of = of_modes(decay, half)

        def gather_state(t, held):
            value = product[rows_of(half * half_rows + t * ROWS), :]
            return [rate_of[n] * held[n] + value for n in range(modes)]

        held = lax.fori_loop(
            0,
            length,
            gather_state,
            [jnp.zeros((ROWS, LANES), jnp.float32)] * modes,
            unroll=8,
        )
        own_state[half] = jnp.concatenate(held, axis=0).astype(jnp.bfloat16)

    def mate_copy(half):
        return pltpu.make_async_remote_copy(
            src_ref=own_state.at[half],
            dst_ref=mate_state.at[half],
            send_sem=mate_send.at[half],
            recv_sem=mate_recv.at[half],
            device_id={"seq": mate},
            device_id_type=MESH,
        )

    find_state(1 - side)
    mate_copy(1 - side).start()
    block_decay[...] = jnp.exp(-float(length) * rates[...])
    pair_decay[...] = block_decay[...] * block_decay[...]
    find_state(side)

    @pl.when(side == 0)
    def _():
        mate_copy(0).start()

    def state_copy(sender, later):
        return pltpu.make_async_remote_copy(
            src_ref=pair_state,
            dst_ref=states.at[sender],
            send_sem=state_send.at[later],
            recv_sem=state_recv.at[sender],
            device_id={"seq": 2 * later + side},
            device_id_type=MESH,
        )

    def for_later(action):
        def step(later, _):
            action(state_copy(pair, later))
            return 0

        lax.fori_loop(pair + 1, pair_count, step, 0)

    mate_copy(side).wait_recv()
    own_part = own_state[side].astype(jnp.float32)
    mate_part = mate_state[side].astype(jnp.float32)
    scale = block_decay[rows_of(side * mode_rows, mode_rows), :]
    even = jnp.where(side == 0, own_part, mate_part)
    odd = jnp.where(side == 0, mate_part, own_part)
    pair_state[...] = (scale * even + odd).astype(jnp.bfloat16)
    for_later(lambda copy: copy.start())
    mix_streams((0,), put_q)
    take_params(1, weights)

    @pl.when(side == 1)
    def _():
        mate_copy(0).wait_recv()
        for half in range(half_count):
            start[half * mode_rows : (half + 1) * mode_rows, :] = mate_state[half].astype(
                jnp.float32
            )

    @pl.when(side == 0)
    def _():
        start[...] = jnp.zeros(start.shape, jnp.float32)

    for half in range(half_count):
        rate_of = of_modes(decay, half)
        weight_of = of_modes(weights, half)

        def convolve(t, held, half=half, rate_of=rate_of, weight_of=weight_of):
            at = rows_of(half * half_rows + t * ROWS)
            value = product[at, :]
            held = [rate_of[n] * held[n] + value for n in range(modes)]
            local[at, :] = tree_sum([weight_of[n] * held[n] for n in range(modes)])
            return held

        lax.fori_loop(0, length, convolve, of_modes(start, half), unroll=4)

    prefix_copy = pltpu.make_async_remote_copy(
        src_ref=prefix,
        dst_ref=mate_prefix,
        send_sem=prefix_send,
        recv_sem=prefix_recv,
        device_id={"seq": mate},
        device_id_type=MESH,
    )
    prefix[...] = jnp.zeros(prefix.shape, jnp.float32)

    def take_state(sender, _):
        state_copy(sender, sender).wait_recv()
        prefix[...] = prefix[...] * pair_decay[rows_of(side * mode_rows, mode_rows), :] + states[
            sender
        ].astype(jnp.float32)
        return 0

    lax.fori_loop(0, pair, take_state, 0)

    @pl.when(pair > 0)
    def _():
        prefix_copy.start()

    def put_gated(at, skip_here, long_part):
        long_part = long_part.astype(jnp.bfloat16).astype(jnp.float32)
        local[at, :] = mixed_q[at, :] * (long_part + skip_here * product[at, :])

    def put_out(half):
        for row in range(ROWS):
            gated = local[pl.ds(half * half_rows + row, length, stride=ROWS), :].astype(jnp.bfloat16)
            first_channel = pl.multiple_of((half * ROWS + row) * LANES, LANES)
            out[pl.ds(first_channel, LANES), :] = gated.T

    @pl.when(pair == 0)
    def _():
        for half in range(half_count):
            skip_here = skip[rows_of(half * ROWS), :]

            def finish(t, _, half=half, skip_here=skip_here):
                at = rows_of(half * half_rows + t * ROWS)
                put_gated(at, skip_here, local[at, :])
                return 0

            lax.fori_loop(0, length, finish, 0, unroll=8)
            put_out(half)

    @pl.when(pair > 0)
    def _():
        for order in range(2):
            half = side if order == 0 else 1 - side
            here = rows_of(half * mode_rows, mode_rows)
            if order == 0:
                carry[...] = prefix[...] * weights[here, :]
            else:
                prefix_copy.wait_recv()
                carry[...] = mate_prefix[...] * weights[here, :]

            @pl.when(side == 1)
            def _(here=here):
                carry[...] = carry[...] * block_decay[here, :]

            rate_of = of_modes(decay, half)
            skip_here = skip[rows_of(half * ROWS), :]

            def finish(t, held, half=half, rate_of=rate_of, skip_here=skip_here):
                at = rows_of(half * half_rows + t * ROWS)
                held = [rate_of[n] * held[n] for n in range(modes)]
                put_gated(at, skip_here, local[at, :] + tree_sum(held))
                return held

            lax.fori_loop(0, length, finish, of_modes(carry, 0), unroll=4)
            put_out(half)

    def drain_params(step, _):
        for kind in range(2):
            param_copy(kind, step).wait_send()
        return 0

    lax.fori_loop(1, seq_count, drain_params, 0)

    @pl.when(me < seq_count - 1)
    def _():
        for s in range(3):
            halo_copy(s).wait_send()

    mate_copy(1 - side).wait_send()

    @pl.when(side == 0)
    def _():
        mate_copy(0).wait_send()

    for_later(lambda copy: copy.wait_send())

    @pl.when(pair > 0)
    def _():
        prefix_copy.wait_send()


def tree_sum(terms):
    while len(terms) > 1:
        terms = [terms[i] + terms[i + 1] for i in range(0, len(terms), 2)]
    return terms[0]


def body(projected, short_taps, skip_gain, residue, decay_rate):
    seq_count = lax.axis_size("seq")
    _, width, length = projected.shape
    filters, modes = residue.shape
    block_count = width // LANES
    half_count = block_count // ROWS
    assert half_count == 2 and seq_count % 2 == 0
    call = functools.partial(kernel, seq_count, modes, half_count, length, filters)
    hbm = pl.BlockSpec(memory_space=pltpu.HBM)
    mode_rows = modes * ROWS
    f32, bf16 = jnp.float32, jnp.bfloat16
    dma = pltpu.SemaphoreType.DMA
    return pl.pallas_call(
        call,
        out_shape=pltpu.VMEM((width, length), bf16),
        in_specs=[hbm] * 5,
        out_specs=pl.BlockSpec(memory_space=pltpu.VMEM),
        scratch_shapes=[
            pltpu.VMEM((modes, filters), f32),
            pltpu.VMEM((modes, filters), f32),
            pltpu.VMEM((3, width, length), bf16),
            pltpu.VMEM((3, 3, width), f32),
            pltpu.VMEM((block_count, LANES), f32),
            pltpu.VMEM((9, block_count, LANES), f32),
            pltpu.VMEM((3 * length * block_count, LANES), f32),
            pltpu.VMEM((length * block_count, LANES), f32),
            pltpu.VMEM((length * block_count, LANES), f32),
            pltpu.VMEM((length * block_count, LANES), f32),
            pltpu.VMEM((2, modes, filters), f32),
            pltpu.VMEM((seq_count, 2, modes, filters), f32),
            pltpu.VMEM((half_count * mode_rows, LANES), f32),
            pltpu.VMEM((half_count * mode_rows, LANES), f32),
            pltpu.VMEM((half_count * mode_rows, LANES), f32),
            pltpu.VMEM((half_count * mode_rows, LANES), f32),
            pltpu.VMEM((half_count * mode_rows, LANES), f32),
            pltpu.VMEM((3, 2, block_count, LANES), bf16),
            pltpu.VMEM((3, 2, block_count, LANES), bf16),
            pltpu.VMEM((half_count, mode_rows, LANES), bf16),
            pltpu.VMEM((half_count, mode_rows, LANES), bf16),
            pltpu.VMEM((mode_rows, LANES), bf16),
            pltpu.VMEM((seq_count // 2, mode_rows, LANES), bf16),
            pltpu.VMEM((mode_rows, LANES), f32),
            pltpu.VMEM((half_count * mode_rows, LANES), f32),
            pltpu.VMEM((mode_rows, LANES), f32),
            pltpu.VMEM((mode_rows, LANES), f32),
            dma((3,)),
            dma((4,)),
            dma((2, seq_count)),
            dma((2, seq_count)),
            dma((3,)),
            dma((3,)),
            dma((2,)),
            dma((2,)),
            dma((seq_count // 2,)),
            dma((seq_count // 2,)),
            dma,
            dma,
        ],
        compiler_params=pltpu.CompilerParams(
            collective_id=0, has_side_effects=True, vmem_limit_bytes=60 * 1024 * 1024
        ),
    )(
        projected,
        short_taps,
        skip_gain.reshape(skip_gain.shape[0] // LANES, LANES),
        residue.T,
        decay_rate.T,
    )


def solution(mesh):
    in_specs = (P(None, "mp", "seq"), P(), P(), P("seq", None), P("seq", None))
    out_specs = P("mp", "seq")
    return jax.shard_map(body, mesh=mesh, in_specs=in_specs, out_specs=out_specs, check_vma=False)
```

```python
import functools

import jax
import jax.numpy as jnp
from jax import lax
from jax.experimental import pallas as pl
from jax.experimental.pallas import tpu as pltpu
from jax.sharding import PartitionSpec as P

MESH = pl.DeviceIdType.MESH
LANES = 128
ROWS = 8


def rows_of(first, count=ROWS):
    return pl.ds(pl.multiple_of(first, ROWS), count)


def kernel(
    seq_count,
    modes,
    half_count,
    length,
    filters,
    projected,
    taps_hbm,
    skip_hbm,
    residue_hbm,
    rate_hbm,
    out,
    residue,
    rate,
    streams,
    taps_raw,
    skip,
    taps,
    laid,
    product,
    mixed_q,
    local,
    own_params,
    params,
    rates,
    weights,
    decay,
    block_decay,
    pair_decay,
    halo_out,
    halo_in,
    own_state,
    mate_state,
    pair_state,
    states,
    carry,
    start,
    prefix,
    mate_prefix,
    in_sem,
    tap_sem,
    param_send,
    param_recv,
    halo_send,
    halo_recv,
    mate_send,
    mate_recv,
    state_send,
    state_recv,
    prefix_send,
    prefix_recv,
):
    me = lax.axis_index("seq")
    group = lax.axis_index("mp")
    block_count = half_count * ROWS
    width = block_count * LANES
    half_rows = length * ROWS
    mode_rows = modes * ROWS
    side = lax.rem(me, 2)
    pair = lax.div(me, 2)
    pair_count = seq_count // 2
    mate = me + 1 - 2 * side

    in_copies = [
        pltpu.make_async_copy(projected.at[s], streams.at[s], in_sem.at[s]) for s in range(3)
    ]
    tap_copy = pltpu.make_async_copy(
        taps_hbm.at[:, :, pl.ds(pl.multiple_of(group * width, LANES), width)],
        taps_raw,
        tap_sem.at[0],
    )
    skip_copy = pltpu.make_async_copy(
        skip_hbm.at[rows_of(group * block_count, block_count)], skip, tap_sem.at[1]
    )
    rate_copy = pltpu.make_async_copy(rate_hbm, rate, tap_sem.at[2])
    residue_copy = pltpu.make_async_copy(residue_hbm, residue, tap_sem.at[3])
    rate_copy.start()
    residue_copy.start()
    for s in (1, 2, 0):
        in_copies[s].start()
    tap_copy.start()
    skip_copy.start()

    def turn(s):
        in_copies[s].wait()
        for block in range(block_count):
            half, row = divmod(block, ROWS)
            laid[pl.ds((s * half_count + half) * half_rows + row, length, stride=ROWS), :] = (
                streams[s, block * LANES : (block + 1) * LANES, :].T.astype(jnp.float32)
            )

    barrier = pltpu.get_barrier_semaphore()

    def greet(step, _):
        peer = lax.rem(me + step, seq_count)
        pl.semaphore_signal(barrier, inc=1, device_id={"seq": peer}, device_id_type=MESH)
        return 0

    lax.fori_loop(1, seq_count, greet, 0)
    rate_copy.wait()
    residue_copy.wait()
    own_params[0] = rate[...]
    own_params[1] = residue[...] * jnp.sqrt(rate[...])
    params[me] = own_params[...]
    turn(1)
    pl.semaphore_wait(barrier, seq_count - 1)

    def param_copy(kind, step):
        peer = lax.rem(me + step, seq_count)
        return pltpu.make_async_remote_copy(
            src_ref=own_params.at[kind],
            dst_ref=params.at[me, kind],
            send_sem=param_send.at[kind, step],
            recv_sem=param_recv.at[kind, step],
            device_id={"seq": peer},
            device_id_type=MESH,
        )

    def send_params(kind):
        def send(step, _):
            param_copy(kind, step).start()
            return 0

        lax.fori_loop(1, seq_count, send, 0)

    send_params(0)

    def laid_row(s, half, t):
        return laid[rows_of((s * half_count + half) * half_rows + t * ROWS), :]

    turn(2)

    def halo_copy(s):
        return pltpu.make_async_remote_copy(
            src_ref=halo_out.at[s],
            dst_ref=halo_in.at[s],
            send_sem=halo_send.at[s],
            recv_sem=halo_recv.at[s],
            device_id={"seq": lax.rem(me + 1, seq_count)},
            device_id_type=MESH,
        )

    def send_halo(s):
        for back in range(2):
            pieces = [laid_row(s, half, length - 2 + back) for half in range(half_count)]
            halo_out[s, back] = jnp.concatenate(pieces, axis=0).astype(jnp.bfloat16)

        @pl.when(me < seq_count - 1)
        def _():
            halo_copy(s).start()

    def take_halo(s):
        @pl.when(me > 0)
        def _():
            halo_copy(s).wait_recv()

        @pl.when(me == 0)
        def _():
            halo_in[s] = jnp.zeros(halo_in.shape[1:], halo_in.dtype)

    send_halo(1)
    send_halo(2)
    turn(0)
    send_halo(0)
    send_params(1)
    tap_copy.wait()
    skip_copy.wait()
    for lag in range(3):
        for s in range(3):
            for block in range(block_count):
                taps[lag * 3 + s, block : block + 1, :] = taps_raw[
                    lag, s : s + 1, block * LANES : (block + 1) * LANES
                ]

    def mix_streams(which, put):
        taps_of = [
            [
                [taps[lag * 3 + s, half * ROWS : (half + 1) * ROWS, :] for lag in range(3)]
                for s in which
            ]
            for half in range(half_count)
        ]

        def mix_at(half, t, now, before, earlier):
            put(
                rows_of(half * half_rows + t * ROWS),
                [
                    tap[0] * now[i] + tap[1] * before[i] + tap[2] * earlier[i]
                    for i, tap in enumerate(taps_of[half])
                ],
            )

        for half in range(half_count):

            def mix(t, past, half=half):
                before, earlier = past
                now = [laid_row(s, half, t) for s in which]
                mix_at(half, t, now, before, earlier)
                return now, before

            first = [[laid_row(s, half, t) for s in which] for t in range(2)]
            lax.fori_loop(2, length, mix, (first[1], first[0]), unroll=6)

        for s in which:
            take_halo(s)
        for half in range(half_count):
            past = [
                [
                    halo_in[s, back].astype(jnp.float32)[half * ROWS : (half + 1) * ROWS]
                    for s in which
                ]
                for back in range(2)
            ]
            first = [[laid_row(s, half, t) for s in which] for t in range(2)]
            mix_at(half, 0, first[0], past[1], past[0])
            mix_at(half, 1, first[1], first[0], past[1])

    def put_product(at, mixed):
        product[at, :] = (mixed[0] * mixed[1]).astype(jnp.bfloat16).astype(jnp.float32)

    def put_q(at, mixed):
        mixed_q[at, :] = mixed[0]

    mix_streams((1, 2), put_product)

    def take_params(kind, target):
        def take(step, _):
            param_copy(kind, step).wait_recv()
            return 0

        lax.fori_loop(1, seq_count, take, 0)
        for block in range(block_count):
            half, row = divmod(block, ROWS)
            if filters >= LANES:
                per = filters // LANES
                lane = (block % per) * LANES
                piece = params[block // per, kind, :, lane : lane + LANES]
            else:
                per = LANES // filters
                piece = jnp.concatenate(
                    [params[block * per + part, kind] for part in range(per)], axis=1
                )
            target[pl.ds(half * mode_rows + row, modes, stride=ROWS), :] = piece

    take_params(0, rates)
    decay[...] = jnp.exp(-rates[...])

    def of_modes(ref, half):
        first = half * mode_rows
        return [ref[rows_of(first + n * ROWS), :] for n in range(modes)]

    def find_state(half):
        rate_of = of_modes(decay, half)

        def gather_state(t, held):
            value = product[rows_of(half * half_rows + t * ROWS), :]
            return [rate_of[n] * held[n] + value for n in range(modes)]

        held = lax.fori_loop(
            0,
            length,
            gather_state,
            [jnp.zeros((ROWS, LANES), jnp.float32)] * modes,
            unroll=8,
        )
        own_state[half] = jnp.concatenate(held, axis=0).astype(jnp.bfloat16)

    def mate_copy(half):
        return pltpu.make_async_remote_copy(
            src_ref=own_state.at[half],
            dst_ref=mate_state.at[half],
            send_sem=mate_send.at[half],
            recv_sem=mate_recv.at[half],
            device_id={"seq": mate},
            device_id_type=MESH,
        )

    find_state(1 - side)
    mate_copy(1 - side).start()
    block_decay[...] = jnp.exp(-float(length) * rates[...])
    pair_decay[...] = block_decay[...] * block_decay[...]
    find_state(side)

    @pl.when(side == 0)
    def _():
        mate_copy(0).start()

    def state_copy(sender, later):
        return pltpu.make_async_remote_copy(
            src_ref=pair_state,
            dst_ref=states.at[sender],
            send_sem=state_send.at[later],
            recv_sem=state_recv.at[sender],
            device_id={"seq": 2 * later + side},
            device_id_type=MESH,
        )

    def for_later(action):
        def step(later, _):
            action(state_copy(pair, later))
            return 0

        lax.fori_loop(pair + 1, pair_count, step, 0)

    mix_streams((0,), put_q)
    mate_copy(side).wait_recv()
    own_part = own_state[side].astype(jnp.float32)
    mate_part = mate_state[side].astype(jnp.float32)
    scale = block_decay[rows_of(side * mode_rows, mode_rows), :]
    even = jnp.where(side == 0, own_part, mate_part)
    odd = jnp.where(side == 0, mate_part, own_part)
    pair_state[...] = (scale * even + odd).astype(jnp.bfloat16)
    for_later(lambda copy: copy.start())
    take_params(1, weights)

    start[...] = jnp.zeros(start.shape, jnp.float32)
    for half in (1, 0):

        @pl.when(side == 1)
        def _(half=half):
            if half == 0:
                mate_copy(0).wait_recv()
            start[...] = mate_state[half].astype(jnp.float32)

        rate_of = of_modes(decay, half)
        weight_of = of_modes(weights, half)

        def convolve(t, held, half=half, rate_of=rate_of, weight_of=weight_of):
            at = rows_of(half * half_rows + t * ROWS)
            value = product[at, :]
            held = [rate_of[n] * held[n] + value for n in range(modes)]
            local[at, :] = tree_sum([weight_of[n] * held[n] for n in range(modes)])
            return held

        lax.fori_loop(0, length, convolve, of_modes(start, 0), unroll=4)

    prefix_copy = pltpu.make_async_remote_copy(
        src_ref=prefix,
        dst_ref=mate_prefix,
        send_sem=prefix_send,
        recv_sem=prefix_recv,
        device_id={"seq": mate},
        device_id_type=MESH,
    )
    prefix[...] = jnp.zeros(prefix.shape, jnp.float32)

    def take_state(sender, _):
        state_copy(sender, sender).wait_recv()
        prefix[...] = prefix[...] * pair_decay[rows_of(side * mode_rows, mode_rows), :] + states[
            sender
        ].astype(jnp.float32)
        return 0

    lax.fori_loop(0, pair, take_state, 0)

    @pl.when(pair > 0)
    def _():
        prefix_copy.start()

    def put_gated(at, skip_here, long_part):
        long_part = long_part.astype(jnp.bfloat16).astype(jnp.float32)
        local[at, :] = mixed_q[at, :] * (long_part + skip_here * product[at, :])

    def gated_of(half, row):
        return local[pl.ds(half * half_rows + row, length, stride=ROWS), :].astype(jnp.bfloat16)

    def put_out(half, row, gated):
        first_channel = pl.multiple_of((half * ROWS + row) * LANES, LANES)
        out[pl.ds(first_channel, LANES), :] = gated.T

    @pl.when(pair == 0)
    def _():
        for half in range(half_count):
            skip_here = skip[rows_of(half * ROWS), :]

            def finish(t, _, half=half, skip_here=skip_here):
                at = rows_of(half * half_rows + t * ROWS)
                put_gated(at, skip_here, local[at, :])
                return 0

            lax.fori_loop(0, length, finish, 0, unroll=8)
            for row in range(ROWS):
                put_out(half, row, gated_of(half, row))

    @pl.when(pair > 0)
    def _():
        for order in range(2):
            half = side if order == 0 else 1 - side
            here = rows_of(half * mode_rows, mode_rows)
            if order == 0:
                carry[...] = prefix[...] * weights[here, :]
            else:
                prefix_copy.wait_recv()
                carry[...] = mate_prefix[...] * weights[here, :]

            @pl.when(side == 1)
            def _(here=here):
                carry[...] = carry[...] * block_decay[here, :]

            rate_of = of_modes(decay, half)
            skip_here = skip[rows_of(half * ROWS), :]

            def finish(t, held, half=half, rate_of=rate_of, skip_here=skip_here):
                at = rows_of(half * half_rows + t * ROWS)
                held = [rate_of[n] * held[n] for n in range(modes)]
                put_gated(at, skip_here, local[at, :] + tree_sum(held))
                return held

            if order == 0:
                lax.fori_loop(0, length, finish, of_modes(carry, 0), unroll=4)
                continue

            def finish_some(row, held, finish=finish):
                gated = gated_of(side, row)
                for step in range(length // ROWS):
                    held = finish(row * (length // ROWS) + step, held)
                put_out(side, row, gated)
                return held

            lax.fori_loop(0, ROWS, finish_some, of_modes(carry, 0))
            for row in range(ROWS):
                put_out(half, row, gated_of(half, row))

    def drain_params(step, _):
        for kind in range(2):
            param_copy(kind, step).wait_send()
        return 0

    lax.fori_loop(1, seq_count, drain_params, 0)

    @pl.when(me < seq_count - 1)
    def _():
        for s in range(3):
            halo_copy(s).wait_send()

    mate_copy(1 - side).wait_send()

    @pl.when(side == 0)
    def _():
        mate_copy(0).wait_send()

    for_later(lambda copy: copy.wait_send())

    @pl.when(pair > 0)
    def _():
        prefix_copy.wait_send()


def tree_sum(terms):
    while len(terms) > 1:
        terms = [terms[i] + terms[i + 1] for i in range(0, len(terms), 2)]
    return terms[0]


def body(projected, short_taps, skip_gain, residue, decay_rate):
    seq_count = lax.axis_size("seq")
    _, width, length = projected.shape
    filters, modes = residue.shape
    block_count = width // LANES
    half_count = block_count // ROWS
    assert half_count == 2 and seq_count % 2 == 0
    call = functools.partial(kernel, seq_count, modes, half_count, length, filters)
    hbm = pl.BlockSpec(memory_space=pltpu.HBM)
    mode_rows = modes * ROWS
    f32, bf16 = jnp.float32, jnp.bfloat16
    dma = pltpu.SemaphoreType.DMA
    return pl.pallas_call(
        call,
        out_shape=pltpu.VMEM((width, length), bf16),
        in_specs=[hbm] * 5,
        out_specs=pl.BlockSpec(memory_space=pltpu.VMEM),
        scratch_shapes=[
            pltpu.VMEM((modes, filters), f32),
            pltpu.VMEM((modes, filters), f32),
            pltpu.VMEM((3, width, length), bf16),
            pltpu.VMEM((3, 3, width), f32),
            pltpu.VMEM((block_count, LANES), f32),
            pltpu.VMEM((9, block_count, LANES), f32),
            pltpu.VMEM((3 * length * block_count, LANES), f32),
            pltpu.VMEM((length * block_count, LANES), f32),
            pltpu.VMEM((length * block_count, LANES), f32),
            pltpu.VMEM((length * block_count, LANES), f32),
            pltpu.VMEM((2, modes, filters), f32),
            pltpu.VMEM((seq_count, 2, modes, filters), f32),
            pltpu.VMEM((half_count * mode_rows, LANES), f32),
            pltpu.VMEM((half_count * mode_rows, LANES), f32),
            pltpu.VMEM((half_count * mode_rows, LANES), f32),
            pltpu.VMEM((half_count * mode_rows, LANES), f32),
            pltpu.VMEM((half_count * mode_rows, LANES), f32),
            pltpu.VMEM((3, 2, block_count, LANES), bf16),
            pltpu.VMEM((3, 2, block_count, LANES), bf16),
            pltpu.VMEM((half_count, mode_rows, LANES), bf16),
            pltpu.VMEM((half_count, mode_rows, LANES), bf16),
            pltpu.VMEM((mode_rows, LANES), bf16),
            pltpu.VMEM((seq_count // 2, mode_rows, LANES), bf16),
            pltpu.VMEM((mode_rows, LANES), f32),
            pltpu.VMEM((mode_rows, LANES), f32),
            pltpu.VMEM((mode_rows, LANES), f32),
            pltpu.VMEM((mode_rows, LANES), f32),
            dma((3,)),
            dma((4,)),
            dma((2, seq_count)),
            dma((2, seq_count)),
            dma((3,)),
            dma((3,)),
            dma((2,)),
            dma((2,)),
            dma((seq_count // 2,)),
            dma((seq_count // 2,)),
            dma,
            dma,
        ],
        compiler_params=pltpu.CompilerParams(
            collective_id=0, has_side_effects=True, vmem_limit_bytes=60 * 1024 * 1024
        ),
    )(
        projected,
        short_taps,
        skip_gain.reshape(skip_gain.shape[0] // LANES, LANES),
        residue.T,
        decay_rate.T,
    )


def solution(mesh):
    in_specs = (P(None, "mp", "seq"), P(), P(), P("seq", None), P("seq", None))
    out_specs = P("mp", "seq")
    return jax.shard_map(body, mesh=mesh, in_specs=in_specs, out_specs=out_specs, check_vma=False)
```

```python
import functools

import jax
import jax.numpy as jnp
from jax import lax
from jax.experimental import pallas as pl
from jax.experimental.pallas import tpu as pltpu
from jax.sharding import PartitionSpec as P

MESH = pl.DeviceIdType.MESH
LANES = 128
ROWS = 8


def rows_of(first, count=ROWS):
    return pl.ds(pl.multiple_of(first, ROWS), count)


def kernel(
    seq_count,
    modes,
    half_count,
    length,
    filters,
    projected,
    taps_hbm,
    skip_hbm,
    residue_hbm,
    rate_hbm,
    out,
    residue,
    rate,
    streams,
    taps_raw,
    skip,
    taps,
    laid,
    product,
    mixed_q,
    local,
    own_params,
    params,
    rates,
    weights,
    decay,
    block_decay,
    pair_decay,
    halo_out,
    halo_in,
    own_state,
    mate_state,
    pair_state,
    states,
    carry,
    start,
    prefix,
    mate_prefix,
    in_sem,
    tap_sem,
    param_send,
    param_recv,
    halo_send,
    halo_recv,
    mate_send,
    mate_recv,
    state_send,
    state_recv,
    prefix_send,
    prefix_recv,
):
    me = lax.axis_index("seq")
    group = lax.axis_index("mp")
    block_count = half_count * ROWS
    width = block_count * LANES
    half_rows = length * ROWS
    mode_rows = modes * ROWS
    side = lax.rem(me, 2)
    pair = lax.div(me, 2)
    pair_count = seq_count // 2
    mate = me + 1 - 2 * side

    in_copies = [
        pltpu.make_async_copy(projected.at[s], streams.at[s], in_sem.at[s]) for s in range(3)
    ]
    tap_copy = pltpu.make_async_copy(
        taps_hbm.at[:, :, pl.ds(pl.multiple_of(group * width, LANES), width)],
        taps_raw,
        tap_sem.at[0],
    )
    skip_copy = pltpu.make_async_copy(
        skip_hbm.at[rows_of(group * block_count, block_count)], skip, tap_sem.at[1]
    )
    rate_copy = pltpu.make_async_copy(rate_hbm, rate, tap_sem.at[2])
    residue_copy = pltpu.make_async_copy(residue_hbm, residue, tap_sem.at[3])
    rate_copy.start()
    residue_copy.start()
    for s in (1, 2, 0):
        in_copies[s].start()
    tap_copy.start()
    skip_copy.start()

    def turn(s):
        in_copies[s].wait()
        for block in range(block_count):
            half, row = divmod(block, ROWS)
            laid[pl.ds((s * half_count + half) * half_rows + row, length, stride=ROWS), :] = (
                streams[s, block * LANES : (block + 1) * LANES, :].T.astype(jnp.float32)
            )

    barrier = pltpu.get_barrier_semaphore()

    def greet(step, _):
        peer = lax.rem(me + step, seq_count)
        pl.semaphore_signal(barrier, inc=1, device_id={"seq": peer}, device_id_type=MESH)
        return 0

    lax.fori_loop(1, seq_count, greet, 0)
    rate_copy.wait()
    residue_copy.wait()
    own_params[0] = rate[...]
    own_params[1] = residue[...] * jnp.sqrt(rate[...])
    params[me] = own_params[...]
    turn(1)
    pl.semaphore_wait(barrier, seq_count - 1)

    def param_copy(kind, step):
        peer = lax.rem(me + step, seq_count)
        return pltpu.make_async_remote_copy(
            src_ref=own_params.at[kind],
            dst_ref=params.at[me, kind],
            send_sem=param_send.at[kind, step],
            recv_sem=param_recv.at[kind, step],
            device_id={"seq": peer},
            device_id_type=MESH,
        )

    def send_params(kind):
        def send(step, _):
            param_copy(kind, step).start()
            return 0

        lax.fori_loop(1, seq_count, send, 0)

    send_params(0)

    def laid_row(s, half, t):
        return laid[rows_of((s * half_count + half) * half_rows + t * ROWS), :]

    turn(2)

    def halo_copy(s):
        return pltpu.make_async_remote_copy(
            src_ref=halo_out.at[s],
            dst_ref=halo_in.at[s],
            send_sem=halo_send.at[s],
            recv_sem=halo_recv.at[s],
            device_id={"seq": lax.rem(me + 1, seq_count)},
            device_id_type=MESH,
        )

    def send_halo(s):
        for back in range(2):
            pieces = [laid_row(s, half, length - 2 + back) for half in range(half_count)]
            halo_out[s, back] = jnp.concatenate(pieces, axis=0).astype(jnp.bfloat16)

        @pl.when(me < seq_count - 1)
        def _():
            halo_copy(s).start()

    def take_halo(s):
        @pl.when(me > 0)
        def _():
            halo_copy(s).wait_recv()

        @pl.when(me == 0)
        def _():
            halo_in[s] = jnp.zeros(halo_in.shape[1:], halo_in.dtype)

    send_halo(1)
    send_halo(2)
    turn(0)
    send_halo(0)
    send_params(1)
    tap_copy.wait()
    skip_copy.wait()
    for lag in range(3):
        for s in range(3):
            for block in range(block_count):
                taps[lag * 3 + s, block : block + 1, :] = taps_raw[
                    lag, s : s + 1, block * LANES : (block + 1) * LANES
                ]

    def mix_streams(which, put):
        taps_of = [
            [
                [taps[lag * 3 + s, half * ROWS : (half + 1) * ROWS, :] for lag in range(3)]
                for s in which
            ]
            for half in range(half_count)
        ]

        def mix_at(half, t, now, before, earlier):
            put(
                rows_of(half * half_rows + t * ROWS),
                [
                    tap[0] * now[i] + tap[1] * before[i] + tap[2] * earlier[i]
                    for i, tap in enumerate(taps_of[half])
                ],
            )

        for half in range(half_count):

            def mix(t, past, half=half):
                before, earlier = past
                now = [laid_row(s, half, t) for s in which]
                mix_at(half, t, now, before, earlier)
                return now, before

            first = [[laid_row(s, half, t) for s in which] for t in range(2)]
            lax.fori_loop(2, length, mix, (first[1], first[0]), unroll=6)

        for s in which:
            take_halo(s)
        for half in range(half_count):
            past = [
                [
                    halo_in[s, back].astype(jnp.float32)[half * ROWS : (half + 1) * ROWS]
                    for s in which
                ]
                for back in range(2)
            ]
            first = [[laid_row(s, half, t) for s in which] for t in range(2)]
            mix_at(half, 0, first[0], past[1], past[0])
            mix_at(half, 1, first[1], first[0], past[1])

    def put_product(at, mixed):
        product[at, :] = (mixed[0] * mixed[1]).astype(jnp.bfloat16).astype(jnp.float32)

    def put_q(at, mixed):
        mixed_q[at, :] = mixed[0]

    mix_streams((1, 2), put_product)

    def take_params(kind, target):
        def take(step, _):
            param_copy(kind, step).wait_recv()
            return 0

        lax.fori_loop(1, seq_count, take, 0)
        for block in range(block_count):
            half, row = divmod(block, ROWS)
            if filters >= LANES:
                per = filters // LANES
                lane = (block % per) * LANES
                piece = params[block // per, kind, :, lane : lane + LANES]
            else:
                per = LANES // filters
                piece = jnp.concatenate(
                    [params[block * per + part, kind] for part in range(per)], axis=1
                )
            target[pl.ds(half * mode_rows + row, modes, stride=ROWS), :] = piece

    take_params(0, rates)
    decay[...] = jnp.exp(-rates[...])

    def of_modes(ref, half):
        first = half * mode_rows
        return [ref[rows_of(first + n * ROWS), :] for n in range(modes)]

    def find_state(half):
        rate_of = of_modes(decay, half)

        def gather_state(t, held):
            value = product[rows_of(half * half_rows + t * ROWS), :]
            return [rate_of[n] * held[n] + value for n in range(modes)]

        held = lax.fori_loop(
            0,
            length,
            gather_state,
            [jnp.zeros((ROWS, LANES), jnp.float32)] * modes,
            unroll=8,
        )
        own_state[half] = jnp.concatenate(held, axis=0).astype(jnp.bfloat16)

    def mate_copy(half):
        return pltpu.make_async_remote_copy(
            src_ref=own_state.at[half],
            dst_ref=mate_state.at[half],
            send_sem=mate_send.at[half],
            recv_sem=mate_recv.at[half],
            device_id={"seq": mate},
            device_id_type=MESH,
        )

    find_state(1 - side)
    mate_copy(1 - side).start()
    block_decay[...] = jnp.exp(-float(length) * rates[...])
    pair_decay[...] = block_decay[...] * block_decay[...]
    find_state(side)

    @pl.when(side == 0)
    def _():
        mate_copy(0).start()

    def state_copy(sender, later):
        return pltpu.make_async_remote_copy(
            src_ref=pair_state,
            dst_ref=states.at[sender],
            send_sem=state_send.at[later],
            recv_sem=state_recv.at[sender],
            device_id={"seq": 2 * later + side},
            device_id_type=MESH,
        )

    def for_later(action):
        def step(later, _):
            action(state_copy(pair, later))
            return 0

        lax.fori_loop(pair + 1, pair_count, step, 0)

    mix_streams((0,), put_q)
    mate_copy(side).wait_recv()
    own_part = own_state[side].astype(jnp.float32)
    mate_part = mate_state[side].astype(jnp.float32)
    scale = block_decay[rows_of(side * mode_rows, mode_rows), :]
    even = jnp.where(side == 0, own_part, mate_part)
    odd = jnp.where(side == 0, mate_part, own_part)
    pair_state[...] = (scale * even + odd).astype(jnp.bfloat16)
    for_later(lambda copy: copy.start())
    take_params(1, weights)

    start[...] = jnp.zeros(start.shape, jnp.float32)
    for half in (1, 0):

        @pl.when(side == 1)
        def _(half=half):
            if half == 0:
                mate_copy(0).wait_recv()
            start[...] = mate_state[half].astype(jnp.float32)

        rate_of = of_modes(decay, half)
        weight_of = of_modes(weights, half)

        def convolve(t, held, half=half, rate_of=rate_of, weight_of=weight_of):
            at = rows_of(half * half_rows + t * ROWS)
            value = product[at, :]
            held = [rate_of[n] * held[n] + value for n in range(modes)]
            local[at, :] = tree_sum([weight_of[n] * held[n] for n in range(modes)])
            return held

        lax.fori_loop(0, length, convolve, of_modes(start, 0), unroll=8)

    prefix_copy = pltpu.make_async_remote_copy(
        src_ref=prefix,
        dst_ref=mate_prefix,
        send_sem=prefix_send,
        recv_sem=prefix_recv,
        device_id={"seq": mate},
        device_id_type=MESH,
    )
    prefix[...] = jnp.zeros(prefix.shape, jnp.float32)

    def take_state(sender, _):
        state_copy(sender, sender).wait_recv()
        prefix[...] = prefix[...] * pair_decay[rows_of(side * mode_rows, mode_rows), :] + states[
            sender
        ].astype(jnp.float32)
        return 0

    lax.fori_loop(0, pair, take_state, 0)

    @pl.when(pair > 0)
    def _():
        prefix_copy.start()

    def put_gated(at, skip_here, long_part):
        long_part = long_part.astype(jnp.bfloat16).astype(jnp.float32)
        local[at, :] = mixed_q[at, :] * (long_part + skip_here * product[at, :])

    def gated_of(half, row):
        return local[pl.ds(half * half_rows + row, length, stride=ROWS), :].astype(jnp.bfloat16)

    def put_out(half, row, gated):
        first_channel = pl.multiple_of((half * ROWS + row) * LANES, LANES)
        out[pl.ds(first_channel, LANES), :] = gated.T

    @pl.when(pair == 0)
    def _():
        for half in range(half_count):
            skip_here = skip[rows_of(half * ROWS), :]

            def finish(t, _, half=half, skip_here=skip_here):
                at = rows_of(half * half_rows + t * ROWS)
                put_gated(at, skip_here, local[at, :])
                return 0

            lax.fori_loop(0, length, finish, 0, unroll=8)
            for row in range(ROWS):
                put_out(half, row, gated_of(half, row))

    @pl.when(pair > 0)
    def _():
        for order in range(2):
            half = side if order == 0 else 1 - side
            here = rows_of(half * mode_rows, mode_rows)
            if order == 0:
                carry[...] = prefix[...] * weights[here, :]
            else:
                prefix_copy.wait_recv()
                carry[...] = mate_prefix[...] * weights[here, :]

            @pl.when(side == 1)
            def _(here=here):
                carry[...] = carry[...] * block_decay[here, :]

            rate_of = of_modes(decay, half)
            skip_here = skip[rows_of(half * ROWS), :]

            def finish(t, held, half=half, rate_of=rate_of, skip_here=skip_here):
                at = rows_of(half * half_rows + t * ROWS)
                held = [rate_of[n] * held[n] for n in range(modes)]
                put_gated(at, skip_here, local[at, :] + tree_sum(held))
                return held

            lax.fori_loop(0, length, finish, of_modes(carry, 0), unroll=8)
            for row in range(ROWS):
                put_out(half, row, gated_of(half, row))

    def drain_params(step, _):
        for kind in range(2):
            param_copy(kind, step).wait_send()
        return 0

    lax.fori_loop(1, seq_count, drain_params, 0)

    @pl.when(me < seq_count - 1)
    def _():
        for s in range(3):
            halo_copy(s).wait_send()

    mate_copy(1 - side).wait_send()

    @pl.when(side == 0)
    def _():
        mate_copy(0).wait_send()

    for_later(lambda copy: copy.wait_send())

    @pl.when(pair > 0)
    def _():
        prefix_copy.wait_send()


def tree_sum(terms):
    while len(terms) > 1:
        terms = [terms[i] + terms[i + 1] for i in range(0, len(terms), 2)]
    return terms[0]


def body(projected, short_taps, skip_gain, residue, decay_rate):
    seq_count = lax.axis_size("seq")
    _, width, length = projected.shape
    filters, modes = residue.shape
    block_count = width // LANES
    half_count = block_count // ROWS
    assert half_count == 2 and seq_count % 2 == 0
    call = functools.partial(kernel, seq_count, modes, half_count, length, filters)
    hbm = pl.BlockSpec(memory_space=pltpu.HBM)
    mode_rows = modes * ROWS
    f32, bf16 = jnp.float32, jnp.bfloat16
    dma = pltpu.SemaphoreType.DMA
    return pl.pallas_call(
        call,
        out_shape=pltpu.VMEM((width, length), bf16),
        in_specs=[hbm] * 5,
        out_specs=pl.BlockSpec(memory_space=pltpu.VMEM),
        scratch_shapes=[
            pltpu.VMEM((modes, filters), f32),
            pltpu.VMEM((modes, filters), f32),
            pltpu.VMEM((3, width, length), bf16),
            pltpu.VMEM((3, 3, width), f32),
            pltpu.VMEM((block_count, LANES), f32),
            pltpu.VMEM((9, block_count, LANES), f32),
            pltpu.VMEM((3 * length * block_count, LANES), f32),
            pltpu.VMEM((length * block_count, LANES), f32),
            pltpu.VMEM((length * block_count, LANES), f32),
            pltpu.VMEM((length * block_count, LANES), f32),
            pltpu.VMEM((2, modes, filters), f32),
            pltpu.VMEM((seq_count, 2, modes, filters), f32),
            pltpu.VMEM((half_count * mode_rows, LANES), f32),
            pltpu.VMEM((half_count * mode_rows, LANES), f32),
            pltpu.VMEM((half_count * mode_rows, LANES), f32),
            pltpu.VMEM((half_count * mode_rows, LANES), f32),
            pltpu.VMEM((half_count * mode_rows, LANES), f32),
            pltpu.VMEM((3, 2, block_count, LANES), bf16),
            pltpu.VMEM((3, 2, block_count, LANES), bf16),
            pltpu.VMEM((half_count, mode_rows, LANES), bf16),
            pltpu.VMEM((half_count, mode_rows, LANES), bf16),
            pltpu.VMEM((mode_rows, LANES), bf16),
            pltpu.VMEM((seq_count // 2, mode_rows, LANES), bf16),
            pltpu.VMEM((mode_rows, LANES), f32),
            pltpu.VMEM((mode_rows, LANES), f32),
            pltpu.VMEM((mode_rows, LANES), f32),
            pltpu.VMEM((mode_rows, LANES), f32),
            dma((3,)),
            dma((4,)),
            dma((2, seq_count)),
            dma((2, seq_count)),
            dma((3,)),
            dma((3,)),
            dma((2,)),
            dma((2,)),
            dma((seq_count // 2,)),
            dma((seq_count // 2,)),
            dma,
            dma,
        ],
        compiler_params=pltpu.CompilerParams(
            collective_id=0, has_side_effects=True, vmem_limit_bytes=60 * 1024 * 1024
        ),
    )(
        projected,
        short_taps,
        skip_gain.reshape(skip_gain.shape[0] // LANES, LANES),
        residue.T,
        decay_rate.T,
    )


def solution(mesh):
    in_specs = (P(None, "mp", "seq"), P(), P(), P("seq", None), P("seq", None))
    out_specs = P("mp", "seq")
    return jax.shard_map(body, mesh=mesh, in_specs=in_specs, out_specs=out_specs, check_vma=False)
```

```python
import functools

import jax
import jax.numpy as jnp
from jax import lax
from jax.experimental import pallas as pl
from jax.experimental.pallas import tpu as pltpu
from jax.sharding import PartitionSpec as P

MESH = pl.DeviceIdType.MESH
LANES = 128
ROWS = 8


def rows_of(first, count=ROWS):
    return pl.ds(pl.multiple_of(first, ROWS), count)


def kernel(
    seq_count,
    modes,
    half_count,
    length,
    filters,
    projected,
    taps_hbm,
    skip_hbm,
    residue_hbm,
    rate_hbm,
    out,
    residue,
    rate,
    streams,
    taps_raw,
    skip,
    taps,
    laid,
    product,
    mixed_q,
    local,
    own_params,
    params,
    rates,
    weights,
    decay,
    block_decay,
    pair_decay,
    halo_out,
    halo_in,
    own_state,
    mate_state,
    pair_state,
    states,
    carry,
    start,
    prefix,
    mate_prefix,
    in_sem,
    tap_sem,
    param_send,
    param_recv,
    halo_send,
    halo_recv,
    mate_send,
    mate_recv,
    state_send,
    state_recv,
    prefix_send,
    prefix_recv,
):
    me = lax.axis_index("seq")
    group = lax.axis_index("mp")
    block_count = half_count * ROWS
    width = block_count * LANES
    half_rows = length * ROWS
    mode_rows = modes * ROWS
    side = lax.rem(me, 2)
    pair = lax.div(me, 2)
    pair_count = seq_count // 2
    mate = me + 1 - 2 * side

    in_copies = [
        pltpu.make_async_copy(projected.at[s], streams.at[s], in_sem.at[s]) for s in range(3)
    ]
    tap_copy = pltpu.make_async_copy(
        taps_hbm.at[:, :, pl.ds(pl.multiple_of(group * width, LANES), width)],
        taps_raw,
        tap_sem.at[0],
    )
    skip_copy = pltpu.make_async_copy(
        skip_hbm.at[rows_of(group * block_count, block_count)], skip, tap_sem.at[1]
    )
    rate_copy = pltpu.make_async_copy(rate_hbm, rate, tap_sem.at[2])
    residue_copy = pltpu.make_async_copy(residue_hbm, residue, tap_sem.at[3])
    rate_copy.start()
    residue_copy.start()
    for s in (1, 2, 0):
        in_copies[s].start()
    tap_copy.start()
    skip_copy.start()

    def turn(s):
        in_copies[s].wait()
        for block in range(block_count):
            half, row = divmod(block, ROWS)
            laid[pl.ds((s * half_count + half) * half_rows + row, length, stride=ROWS), :] = (
                streams[s, block * LANES : (block + 1) * LANES, :].T.astype(jnp.float32)
            )

    barrier = pltpu.get_barrier_semaphore()

    def greet(step, _):
        peer = lax.rem(me + step, seq_count)
        pl.semaphore_signal(barrier, inc=1, device_id={"seq": peer}, device_id_type=MESH)
        return 0

    lax.fori_loop(1, seq_count, greet, 0)
    rate_copy.wait()
    residue_copy.wait()
    own_params[0] = rate[...]
    own_params[1] = residue[...] * jnp.sqrt(rate[...])
    params[me] = own_params[...]
    turn(1)
    pl.semaphore_wait(barrier, seq_count - 1)

    def param_copy(kind, step):
        peer = lax.rem(me + step, seq_count)
        return pltpu.make_async_remote_copy(
            src_ref=own_params.at[kind],
            dst_ref=params.at[me, kind],
            send_sem=param_send.at[kind, step],
            recv_sem=param_recv.at[kind, step],
            device_id={"seq": peer},
            device_id_type=MESH,
        )

    def send_params(kind):
        first_side = 1 - lax.div(me, seq_count // 2)
        for target_side in (first_side, 1 - first_side):

            def send(ahead, _, target_side=target_side):
                peer = 2 * lax.rem(pair + ahead, pair_count) + target_side

                @pl.when(peer != me)
                def _():
                    param_copy(kind, lax.rem(peer - me + seq_count, seq_count)).start()

                return 0

            lax.fori_loop(0, pair_count, send, 0)

    send_params(0)

    def laid_row(s, half, t):
        return laid[rows_of((s * half_count + half) * half_rows + t * ROWS), :]

    turn(2)

    def halo_copy(s):
        return pltpu.make_async_remote_copy(
            src_ref=halo_out.at[s],
            dst_ref=halo_in.at[s],
            send_sem=halo_send.at[s],
            recv_sem=halo_recv.at[s],
            device_id={"seq": lax.rem(me + 1, seq_count)},
            device_id_type=MESH,
        )

    def send_halo(s):
        for back in range(2):
            pieces = [laid_row(s, half, length - 2 + back) for half in range(half_count)]
            halo_out[s, back] = jnp.concatenate(pieces, axis=0).astype(jnp.bfloat16)

        @pl.when(me < seq_count - 1)
        def _():
            halo_copy(s).start()

    def take_halo(s):
        @pl.when(me > 0)
        def _():
            halo_copy(s).wait_recv()

        @pl.when(me == 0)
        def _():
            halo_in[s] = jnp.zeros(halo_in.shape[1:], halo_in.dtype)

    send_halo(1)
    send_halo(2)
    turn(0)
    send_halo(0)
    send_params(1)
    tap_copy.wait()
    skip_copy.wait()
    for lag in range(3):
        for s in range(3):
            for block in range(block_count):
                taps[lag * 3 + s, block : block + 1, :] = taps_raw[
                    lag, s : s + 1, block * LANES : (block + 1) * LANES
                ]

    def mix_streams(which, put):
        taps_of = [
            [
                [taps[lag * 3 + s, half * ROWS : (half + 1) * ROWS, :] for lag in range(3)]
                for s in which
            ]
            for half in range(half_count)
        ]

        def mix_at(half, t, now, before, earlier):
            put(
                rows_of(half * half_rows + t * ROWS),
                [
                    tap[0] * now[i] + tap[1] * before[i] + tap[2] * earlier[i]
                    for i, tap in enumerate(taps_of[half])
                ],
            )

        for half in range(half_count):

            def mix(t, past, half=half):
                before, earlier = past
                now = [laid_row(s, half, t) for s in which]
                mix_at(half, t, now, before, earlier)
                return now, before

            first = [[laid_row(s, half, t) for s in which] for t in range(2)]
            lax.fori_loop(2, length, mix, (first[1], first[0]), unroll=6)

        for s in which:
            take_halo(s)
        for half in range(half_count):
            past = [
                [
                    halo_in[s, back].astype(jnp.float32)[half * ROWS : (half + 1) * ROWS]
                    for s in which
                ]
                for back in range(2)
            ]
            first = [[laid_row(s, half, t) for s in which] for t in range(2)]
            mix_at(half, 0, first[0], past[1], past[0])
            mix_at(half, 1, first[1], first[0], past[1])

    def put_product(at, mixed):
        product[at, :] = (mixed[0] * mixed[1]).astype(jnp.bfloat16).astype(jnp.float32)

    def put_q(at, mixed):
        mixed_q[at, :] = mixed[0]

    mix_streams((1, 2), put_product)

    def take_params(kind, target, half):
        def take(sender, _):
            @pl.when(sender != me)
            def _():
                param_copy(kind, lax.rem(me - sender + seq_count, seq_count)).wait_recv()

            return 0

        first_sender = half * (seq_count // 2)
        lax.fori_loop(first_sender, first_sender + seq_count // 2, take, 0)
        for row in range(ROWS):
            if filters >= LANES:
                per = filters // LANES
                lane = (row % per) * LANES
                piece = params[first_sender + row // per, kind, :, lane : lane + LANES]
            else:
                per = LANES // filters
                piece = jnp.concatenate(
                    [params[first_sender + row * per + part, kind] for part in range(per)], axis=1
                )
            target[pl.ds(half * mode_rows + row, modes, stride=ROWS), :] = piece

    def of_modes(ref, half):
        first = half * mode_rows
        return [ref[rows_of(first + n * ROWS), :] for n in range(modes)]

    def find_state(half):
        here = rows_of(half * mode_rows, mode_rows)
        take_params(0, rates, half)
        decay[here, :] = jnp.exp(-rates[here, :])
        rate_of = of_modes(decay, half)

        def gather_state(t, held):
            value = product[rows_of(half * half_rows + t * ROWS), :]
            return [rate_of[n] * held[n] + value for n in range(modes)]

        held = lax.fori_loop(
            0,
            length,
            gather_state,
            [jnp.zeros((ROWS, LANES), jnp.float32)] * modes,
            unroll=8,
        )
        own_state[half] = jnp.concatenate(held, axis=0).astype(jnp.bfloat16)

    def mate_copy(half):
        return pltpu.make_async_remote_copy(
            src_ref=own_state.at[half],
            dst_ref=mate_state.at[half],
            send_sem=mate_send.at[half],
            recv_sem=mate_recv.at[half],
            device_id={"seq": mate},
            device_id_type=MESH,
        )

    find_state(1 - side)
    mate_copy(1 - side).start()
    find_state(side)

    @pl.when(side == 0)
    def _():
        mate_copy(0).start()

    def state_copy(sender, later):
        return pltpu.make_async_remote_copy(
            src_ref=pair_state,
            dst_ref=states.at[sender],
            send_sem=state_send.at[later],
            recv_sem=state_recv.at[sender],
            device_id={"seq": 2 * later + side},
            device_id_type=MESH,
        )

    def for_later(action):
        def step(later, _):
            action(state_copy(pair, later))
            return 0

        lax.fori_loop(pair + 1, pair_count, step, 0)

    block_decay[...] = jnp.exp(-float(length) * rates[...])
    pair_decay[...] = block_decay[...] * block_decay[...]
    mix_streams((0,), put_q)
    mate_copy(side).wait_recv()
    own_part = own_state[side].astype(jnp.float32)
    mate_part = mate_state[side].astype(jnp.float32)
    scale = block_decay[rows_of(side * mode_rows, mode_rows), :]
    even = jnp.where(side == 0, own_part, mate_part)
    odd = jnp.where(side == 0, mate_part, own_part)
    pair_state[...] = (scale * even + odd).astype(jnp.bfloat16)
    for_later(lambda copy: copy.start())
    for half in range(half_count):
        take_params(1, weights, half)

    start[...] = jnp.zeros(start.shape, jnp.float32)
    for half in (1, 0):

        @pl.when(side == 1)
        def _(half=half):
            if half == 0:
                mate_copy(0).wait_recv()
            start[...] = mate_state[half].astype(jnp.float32)

        rate_of = of_modes(decay, half)
        weight_of = of_modes(weights, half)

        def convolve(t, held, half=half, rate_of=rate_of, weight_of=weight_of):
            at = rows_of(half * half_rows + t * ROWS)
            value = product[at, :]
            held = [rate_of[n] * held[n] + value for n in range(modes)]
            local[at, :] = tree_sum([weight_of[n] * held[n] for n in range(modes)])
            return held

        lax.fori_loop(0, length, convolve, of_modes(start, 0), unroll=8)

    prefix_copy = pltpu.make_async_remote_copy(
        src_ref=prefix,
        dst_ref=mate_prefix,
        send_sem=prefix_send,
        recv_sem=prefix_recv,
        device_id={"seq": mate},
        device_id_type=MESH,
    )
    prefix[...] = jnp.zeros(prefix.shape, jnp.float32)

    def take_state(sender, _):
        state_copy(sender, sender).wait_recv()
        prefix[...] = prefix[...] * pair_decay[rows_of(side * mode_rows, mode_rows), :] + states[
            sender
        ].astype(jnp.float32)
        return 0

    lax.fori_loop(0, pair, take_state, 0)

    @pl.when(pair > 0)
    def _():
        prefix_copy.start()

    def put_gated(at, skip_here, long_part):
        long_part = long_part.astype(jnp.bfloat16).astype(jnp.float32)
        local[at, :] = mixed_q[at, :] * (long_part + skip_here * product[at, :])

    def gated_of(half, row):
        return local[pl.ds(half * half_rows + row, length, stride=ROWS), :].astype(jnp.bfloat16)

    def put_out(half, row, gated):
        first_channel = pl.multiple_of((half * ROWS + row) * LANES, LANES)
        out[pl.ds(first_channel, LANES), :] = gated.T

    @pl.when(pair == 0)
    def _():
        for half in range(half_count):
            skip_here = skip[rows_of(half * ROWS), :]

            def finish(t, _, half=half, skip_here=skip_here):
                at = rows_of(half * half_rows + t * ROWS)
                put_gated(at, skip_here, local[at, :])
                return 0

            lax.fori_loop(0, length, finish, 0, unroll=8)
            for row in range(ROWS):
                put_out(half, row, gated_of(half, row))

    @pl.when(pair > 0)
    def _():
        for order in range(2):
            half = side if order == 0 else 1 - side
            here = rows_of(half * mode_rows, mode_rows)
            if order == 0:
                carry[...] = prefix[...] * weights[here, :]
            else:
                prefix_copy.wait_recv()
                carry[...] = mate_prefix[...] * weights[here, :]

            @pl.when(side == 1)
            def _(here=here):
                carry[...] = carry[...] * block_decay[here, :]

            rate_of = of_modes(decay, half)
            skip_here = skip[rows_of(half * ROWS), :]

            def finish(t, held, half=half, rate_of=rate_of, skip_here=skip_here):
                at = rows_of(half * half_rows + t * ROWS)
                held = [rate_of[n] * held[n] for n in range(modes)]
                put_gated(at, skip_here, local[at, :] + tree_sum(held))
                return held

            lax.fori_loop(0, length, finish, of_modes(carry, 0), unroll=8)
            for row in range(ROWS):
                put_out(half, row, gated_of(half, row))

    def drain_params(step, _):
        for kind in range(2):
            param_copy(kind, step).wait_send()
        return 0

    lax.fori_loop(1, seq_count, drain_params, 0)

    @pl.when(me < seq_count - 1)
    def _():
        for s in range(3):
            halo_copy(s).wait_send()

    mate_copy(1 - side).wait_send()

    @pl.when(side == 0)
    def _():
        mate_copy(0).wait_send()

    for_later(lambda copy: copy.wait_send())

    @pl.when(pair > 0)
    def _():
        prefix_copy.wait_send()


def tree_sum(terms):
    while len(terms) > 1:
        terms = [terms[i] + terms[i + 1] for i in range(0, len(terms), 2)]
    return terms[0]


def body(projected, short_taps, skip_gain, residue, decay_rate):
    seq_count = lax.axis_size("seq")
    _, width, length = projected.shape
    filters, modes = residue.shape
    block_count = width // LANES
    half_count = block_count // ROWS
    assert half_count == 2 and seq_count % 2 == 0
    call = functools.partial(kernel, seq_count, modes, half_count, length, filters)
    hbm = pl.BlockSpec(memory_space=pltpu.HBM)
    mode_rows = modes * ROWS
    f32, bf16 = jnp.float32, jnp.bfloat16
    dma = pltpu.SemaphoreType.DMA
    return pl.pallas_call(
        call,
        out_shape=pltpu.VMEM((width, length), bf16),
        in_specs=[hbm] * 5,
        out_specs=pl.BlockSpec(memory_space=pltpu.VMEM),
        scratch_shapes=[
            pltpu.VMEM((modes, filters), f32),
            pltpu.VMEM((modes, filters), f32),
            pltpu.VMEM((3, width, length), bf16),
            pltpu.VMEM((3, 3, width), f32),
            pltpu.VMEM((block_count, LANES), f32),
            pltpu.VMEM((9, block_count, LANES), f32),
            pltpu.VMEM((3 * length * block_count, LANES), f32),
            pltpu.VMEM((length * block_count, LANES), f32),
            pltpu.VMEM((length * block_count, LANES), f32),
            pltpu.VMEM((length * block_count, LANES), f32),
            pltpu.VMEM((2, modes, filters), f32),
            pltpu.VMEM((seq_count, 2, modes, filters), f32),
            pltpu.VMEM((half_count * mode_rows, LANES), f32),
            pltpu.VMEM((half_count * mode_rows, LANES), f32),
            pltpu.VMEM((half_count * mode_rows, LANES), f32),
            pltpu.VMEM((half_count * mode_rows, LANES), f32),
            pltpu.VMEM((half_count * mode_rows, LANES), f32),
            pltpu.VMEM((3, 2, block_count, LANES), bf16),
            pltpu.VMEM((3, 2, block_count, LANES), bf16),
            pltpu.VMEM((half_count, mode_rows, LANES), bf16),
            pltpu.VMEM((half_count, mode_rows, LANES), bf16),
            pltpu.VMEM((mode_rows, LANES), bf16),
            pltpu.VMEM((seq_count // 2, mode_rows, LANES), bf16),
            pltpu.VMEM((mode_rows, LANES), f32),
            pltpu.VMEM((mode_rows, LANES), f32),
            pltpu.VMEM((mode_rows, LANES), f32),
            pltpu.VMEM((mode_rows, LANES), f32),
            dma((3,)),
            dma((4,)),
            dma((2, seq_count)),
            dma((2, seq_count)),
            dma((3,)),
            dma((3,)),
            dma((2,)),
            dma((2,)),
            dma((seq_count // 2,)),
            dma((seq_count // 2,)),
            dma,
            dma,
        ],
        compiler_params=pltpu.CompilerParams(
            collective_id=0, has_side_effects=True, vmem_limit_bytes=60 * 1024 * 1024
        ),
    )(
        projected,
        short_taps,
        skip_gain.reshape(skip_gain.shape[0] // LANES, LANES),
        residue.T,
        decay_rate.T,
    )


def solution(mesh):
    in_specs = (P(None, "mp", "seq"), P(), P(), P("seq", None), P("seq", None))
    out_specs = P("mp", "seq")
    return jax.shard_map(body, mesh=mesh, in_specs=in_specs, out_specs=out_specs, check_vma=False)
```

```python
import functools

import jax
import jax.numpy as jnp
from jax import lax
from jax.experimental import pallas as pl
from jax.experimental.pallas import tpu as pltpu
from jax.sharding import PartitionSpec as P

MESH = pl.DeviceIdType.MESH
LANES = 128
ROWS = 8


def rows_of(first, count=ROWS):
    return pl.ds(pl.multiple_of(first, ROWS), count)


def kernel(
    seq_count,
    modes,
    half_count,
    length,
    filters,
    projected,
    taps_hbm,
    skip_hbm,
    residue_hbm,
    rate_hbm,
    out,
    residue,
    rate,
    streams,
    taps_raw,
    skip,
    taps,
    laid,
    product,
    mixed_q,
    local,
    own_params,
    params,
    rates,
    weights,
    decay,
    block_decay,
    pair_decay,
    halo_out,
    halo_in,
    own_state,
    mate_state,
    pair_state,
    states,
    carry,
    start,
    prefix,
    mate_prefix,
    in_sem,
    tap_sem,
    param_send,
    param_recv,
    halo_send,
    halo_recv,
    mate_send,
    mate_recv,
    state_send,
    state_recv,
    prefix_send,
    prefix_recv,
):
    me = lax.axis_index("seq")
    group = lax.axis_index("mp")
    block_count = half_count * ROWS
    width = block_count * LANES
    half_rows = length * ROWS
    mode_rows = modes * ROWS
    side = lax.rem(me, 2)
    pair = lax.div(me, 2)
    pair_count = seq_count // 2
    mate = me + 1 - 2 * side

    in_copies = [
        pltpu.make_async_copy(projected.at[s], streams.at[s], in_sem.at[s]) for s in range(3)
    ]
    tap_copy = pltpu.make_async_copy(
        taps_hbm.at[:, :, pl.ds(pl.multiple_of(group * width, LANES), width)],
        taps_raw,
        tap_sem.at[0],
    )
    skip_copy = pltpu.make_async_copy(
        skip_hbm.at[rows_of(group * block_count, block_count)], skip, tap_sem.at[1]
    )
    rate_copy = pltpu.make_async_copy(rate_hbm, rate, tap_sem.at[2])
    residue_copy = pltpu.make_async_copy(residue_hbm, residue, tap_sem.at[3])
    rate_copy.start()
    residue_copy.start()
    for s in (1, 2, 0):
        in_copies[s].start()
    tap_copy.start()
    skip_copy.start()

    def turn(s):
        in_copies[s].wait()
        for block in range(block_count):
            half, row = divmod(block, ROWS)
            laid[pl.ds((s * half_count + half) * half_rows + row, length, stride=ROWS), :] = (
                streams[s, block * LANES : (block + 1) * LANES, :].T.astype(jnp.float32)
            )

    barrier = pltpu.get_barrier_semaphore()

    def greet(step, _):
        peer = lax.rem(me + step, seq_count)
        pl.semaphore_signal(barrier, inc=1, device_id={"seq": peer}, device_id_type=MESH)
        return 0

    lax.fori_loop(1, seq_count, greet, 0)
    rate_copy.wait()
    residue_copy.wait()
    own_params[0] = rate[...]
    own_params[1] = residue[...] * jnp.sqrt(rate[...])
    params[me] = own_params[...]
    turn(1)
    pl.semaphore_wait(barrier, seq_count - 1)

    def param_copy(kind, step):
        peer = lax.rem(me + step, seq_count)
        return pltpu.make_async_remote_copy(
            src_ref=own_params.at[kind],
            dst_ref=params.at[me, kind],
            send_sem=param_send.at[kind, step],
            recv_sem=param_recv.at[kind, step],
            device_id={"seq": peer},
            device_id_type=MESH,
        )

    def send_params(kind):
        first_side = 1 - lax.div(me, seq_count // 2)
        for target_side in (first_side, 1 - first_side):

            def send(ahead, _, target_side=target_side):
                peer = 2 * lax.rem(pair + ahead, pair_count) + target_side

                @pl.when(peer != me)
                def _():
                    param_copy(kind, lax.rem(peer - me + seq_count, seq_count)).start()

                return 0

            lax.fori_loop(0, pair_count, send, 0)

    send_params(0)

    def laid_row(s, half, t):
        return laid[rows_of((s * half_count + half) * half_rows + t * ROWS), :]

    turn(2)

    def halo_copy(s):
        return pltpu.make_async_remote_copy(
            src_ref=halo_out.at[s],
            dst_ref=halo_in.at[s],
            send_sem=halo_send.at[s],
            recv_sem=halo_recv.at[s],
            device_id={"seq": lax.rem(me + 1, seq_count)},
            device_id_type=MESH,
        )

    def send_halo(s):
        for back in range(2):
            pieces = [laid_row(s, half, length - 2 + back) for half in range(half_count)]
            halo_out[s, back] = jnp.concatenate(pieces, axis=0).astype(jnp.bfloat16)

        @pl.when(me < seq_count - 1)
        def _():
            halo_copy(s).start()

    def take_halo(s):
        @pl.when(me > 0)
        def _():
            halo_copy(s).wait_recv()

        @pl.when(me == 0)
        def _():
            halo_in[s] = jnp.zeros(halo_in.shape[1:], halo_in.dtype)

    send_halo(1)
    send_halo(2)
    turn(0)
    send_halo(0)
    send_params(1)
    tap_copy.wait()
    skip_copy.wait()
    for lag in range(3):
        for s in range(3):
            for block in range(block_count):
                taps[lag * 3 + s, block : block + 1, :] = taps_raw[
                    lag, s : s + 1, block * LANES : (block + 1) * LANES
                ]

    def mix_streams(which, put):
        taps_of = [
            [
                [taps[lag * 3 + s, half * ROWS : (half + 1) * ROWS, :] for lag in range(3)]
                for s in which
            ]
            for half in range(half_count)
        ]

        def mix_at(half, t, now, before, earlier):
            put(
                rows_of(half * half_rows + t * ROWS),
                [
                    tap[0] * now[i] + tap[1] * before[i] + tap[2] * earlier[i]
                    for i, tap in enumerate(taps_of[half])
                ],
            )

        for half in range(half_count):

            def mix(t, past, half=half):
                before, earlier = past
                now = [laid_row(s, half, t) for s in which]
                mix_at(half, t, now, before, earlier)
                return now, before

            first = [[laid_row(s, half, t) for s in which] for t in range(2)]
            lax.fori_loop(2, length, mix, (first[1], first[0]), unroll=14)

        for s in which:
            take_halo(s)
        for half in range(half_count):
            past = [
                [
                    halo_in[s, back].astype(jnp.float32)[half * ROWS : (half + 1) * ROWS]
                    for s in which
                ]
                for back in range(2)
            ]
            first = [[laid_row(s, half, t) for s in which] for t in range(2)]
            mix_at(half, 0, first[0], past[1], past[0])
            mix_at(half, 1, first[1], first[0], past[1])

    def put_product(at, mixed):
        product[at, :] = (mixed[0] * mixed[1]).astype(jnp.bfloat16).astype(jnp.float32)

    def put_q(at, mixed):
        mixed_q[at, :] = mixed[0]

    mix_streams((1, 2), put_product)

    def take_params(kind, target, half):
        def take(sender, _):
            @pl.when(sender != me)
            def _():
                param_copy(kind, lax.rem(me - sender + seq_count, seq_count)).wait_recv()

            return 0

        first_sender = half * (seq_count // 2)
        lax.fori_loop(first_sender, first_sender + seq_count // 2, take, 0)
        for row in range(ROWS):
            if filters >= LANES:
                per = filters // LANES
                lane = (row % per) * LANES
                piece = params[first_sender + row // per, kind, :, lane : lane + LANES]
            else:
                per = LANES // filters
                piece = jnp.concatenate(
                    [params[first_sender + row * per + part, kind] for part in range(per)], axis=1
                )
            target[pl.ds(half * mode_rows + row, modes, stride=ROWS), :] = piece

    def of_modes(ref, half):
        first = half * mode_rows
        return [ref[rows_of(first + n * ROWS), :] for n in range(modes)]

    def find_state(half):
        here = rows_of(half * mode_rows, mode_rows)
        take_params(0, rates, half)
        decay[here, :] = jnp.exp(-rates[here, :])
        rate_of = of_modes(decay, half)

        def gather_state(t, held):
            value = product[rows_of(half * half_rows + t * ROWS), :]
            return [rate_of[n] * held[n] + value for n in range(modes)]

        held = lax.fori_loop(
            0,
            length,
            gather_state,
            [jnp.zeros((ROWS, LANES), jnp.float32)] * modes,
            unroll=16,
        )
        own_state[half] = jnp.concatenate(held, axis=0).astype(jnp.bfloat16)

    def mate_copy(half):
        return pltpu.make_async_remote_copy(
            src_ref=own_state.at[half],
            dst_ref=mate_state.at[half],
            send_sem=mate_send.at[half],
            recv_sem=mate_recv.at[half],
            device_id={"seq": mate},
            device_id_type=MESH,
        )

    find_state(1 - side)
    mate_copy(1 - side).start()
    find_state(side)

    @pl.when(side == 0)
    def _():
        mate_copy(0).start()

    def state_copy(sender, later):
        return pltpu.make_async_remote_copy(
            src_ref=pair_state,
            dst_ref=states.at[sender],
            send_sem=state_send.at[later],
            recv_sem=state_recv.at[sender],
            device_id={"seq": 2 * later + side},
            device_id_type=MESH,
        )

    def for_later(action):
        def step(later, _):
            action(state_copy(pair, later))
            return 0

        lax.fori_loop(pair + 1, pair_count, step, 0)

    block_decay[...] = jnp.exp(-float(length) * rates[...])
    pair_decay[...] = block_decay[...] * block_decay[...]
    mix_streams((0,), put_q)
    mate_copy(side).wait_recv()
    own_part = own_state[side].astype(jnp.float32)
    mate_part = mate_state[side].astype(jnp.float32)
    scale = block_decay[rows_of(side * mode_rows, mode_rows), :]
    even = jnp.where(side == 0, own_part, mate_part)
    odd = jnp.where(side == 0, mate_part, own_part)
    pair_state[...] = (scale * even + odd).astype(jnp.bfloat16)
    for_later(lambda copy: copy.start())
    for half in range(half_count):
        take_params(1, weights, half)

    start[...] = jnp.zeros(start.shape, jnp.float32)
    for half in (1, 0):

        @pl.when(side == 1)
        def _(half=half):
            if half == 0:
                mate_copy(0).wait_recv()
            start[...] = mate_state[half].astype(jnp.float32)

        rate_of = of_modes(decay, half)
        weight_of = of_modes(weights, half)

        def convolve(t, held, half=half, rate_of=rate_of, weight_of=weight_of):
            at = rows_of(half * half_rows + t * ROWS)
            value = product[at, :]
            held = [rate_of[n] * held[n] + value for n in range(modes)]
            local[at, :] = tree_sum([weight_of[n] * held[n] for n in range(modes)])
            return held

        lax.fori_loop(0, length, convolve, of_modes(start, 0), unroll=16)

    prefix_copy = pltpu.make_async_remote_copy(
        src_ref=prefix,
        dst_ref=mate_prefix,
        send_sem=prefix_send,
        recv_sem=prefix_recv,
        device_id={"seq": mate},
        device_id_type=MESH,
    )
    prefix[...] = jnp.zeros(prefix.shape, jnp.float32)

    def take_state(sender, _):
        state_copy(sender, sender).wait_recv()
        prefix[...] = prefix[...] * pair_decay[rows_of(side * mode_rows, mode_rows), :] + states[
            sender
        ].astype(jnp.float32)
        return 0

    lax.fori_loop(0, pair, take_state, 0)

    @pl.when(pair > 0)
    def _():
        prefix_copy.start()

    def put_gated(at, skip_here, long_part):
        long_part = long_part.astype(jnp.bfloat16).astype(jnp.float32)
        local[at, :] = mixed_q[at, :] * (long_part + skip_here * product[at, :])

    def gated_of(half, row):
        return local[pl.ds(half * half_rows + row, length, stride=ROWS), :].astype(jnp.bfloat16)

    def put_out(half, row, gated):
        first_channel = pl.multiple_of((half * ROWS + row) * LANES, LANES)
        out[pl.ds(first_channel, LANES), :] = gated.T

    @pl.when(pair == 0)
    def _():
        for half in range(half_count):
            skip_here = skip[rows_of(half * ROWS), :]

            def finish(t, _, half=half, skip_here=skip_here):
                at = rows_of(half * half_rows + t * ROWS)
                put_gated(at, skip_here, local[at, :])
                return 0

            lax.fori_loop(0, length, finish, 0, unroll=16)
            for row in range(ROWS):
                put_out(half, row, gated_of(half, row))

    @pl.when(pair > 0)
    def _():
        for order in range(2):
            half = side if order == 0 else 1 - side
            here = rows_of(half * mode_rows, mode_rows)
            if order == 0:
                carry[...] = prefix[...] * weights[here, :]
            else:
                prefix_copy.wait_recv()
                carry[...] = mate_prefix[...] * weights[here, :]

            @pl.when(side == 1)
            def _(here=here):
                carry[...] = carry[...] * block_decay[here, :]

            rate_of = of_modes(decay, half)
            skip_here = skip[rows_of(half * ROWS), :]

            def finish(t, held, half=half, rate_of=rate_of, skip_here=skip_here):
                at = rows_of(half * half_rows + t * ROWS)
                held = [rate_of[n] * held[n] for n in range(modes)]
                put_gated(at, skip_here, local[at, :] + tree_sum(held))
                return held

            lax.fori_loop(0, length, finish, of_modes(carry, 0), unroll=16)
            for row in range(ROWS):
                put_out(half, row, gated_of(half, row))

    def drain_params(step, _):
        for kind in range(2):
            param_copy(kind, step).wait_send()
        return 0

    lax.fori_loop(1, seq_count, drain_params, 0)

    @pl.when(me < seq_count - 1)
    def _():
        for s in range(3):
            halo_copy(s).wait_send()

    mate_copy(1 - side).wait_send()

    @pl.when(side == 0)
    def _():
        mate_copy(0).wait_send()

    for_later(lambda copy: copy.wait_send())

    @pl.when(pair > 0)
    def _():
        prefix_copy.wait_send()


def tree_sum(terms):
    while len(terms) > 1:
        terms = [terms[i] + terms[i + 1] for i in range(0, len(terms), 2)]
    return terms[0]


def body(projected, short_taps, skip_gain, residue, decay_rate):
    seq_count = lax.axis_size("seq")
    _, width, length = projected.shape
    filters, modes = residue.shape
    block_count = width // LANES
    half_count = block_count // ROWS
    assert half_count == 2 and seq_count % 2 == 0
    call = functools.partial(kernel, seq_count, modes, half_count, length, filters)
    hbm = pl.BlockSpec(memory_space=pltpu.HBM)
    mode_rows = modes * ROWS
    f32, bf16 = jnp.float32, jnp.bfloat16
    dma = pltpu.SemaphoreType.DMA
    return pl.pallas_call(
        call,
        out_shape=pltpu.VMEM((width, length), bf16),
        in_specs=[hbm] * 5,
        out_specs=pl.BlockSpec(memory_space=pltpu.VMEM),
        scratch_shapes=[
            pltpu.VMEM((modes, filters), f32),
            pltpu.VMEM((modes, filters), f32),
            pltpu.VMEM((3, width, length), bf16),
            pltpu.VMEM((3, 3, width), f32),
            pltpu.VMEM((block_count, LANES), f32),
            pltpu.VMEM((9, block_count, LANES), f32),
            pltpu.VMEM((3 * length * block_count, LANES), f32),
            pltpu.VMEM((length * block_count, LANES), f32),
            pltpu.VMEM((length * block_count, LANES), f32),
            pltpu.VMEM((length * block_count, LANES), f32),
            pltpu.VMEM((2, modes, filters), f32),
            pltpu.VMEM((seq_count, 2, modes, filters), f32),
            pltpu.VMEM((half_count * mode_rows, LANES), f32),
            pltpu.VMEM((half_count * mode_rows, LANES), f32),
            pltpu.VMEM((half_count * mode_rows, LANES), f32),
            pltpu.VMEM((half_count * mode_rows, LANES), f32),
            pltpu.VMEM((half_count * mode_rows, LANES), f32),
            pltpu.VMEM((3, 2, block_count, LANES), bf16),
            pltpu.VMEM((3, 2, block_count, LANES), bf16),
            pltpu.VMEM((half_count, mode_rows, LANES), bf16),
            pltpu.VMEM((half_count, mode_rows, LANES), bf16),
            pltpu.VMEM((mode_rows, LANES), bf16),
            pltpu.VMEM((seq_count // 2, mode_rows, LANES), bf16),
            pltpu.VMEM((mode_rows, LANES), f32),
            pltpu.VMEM((mode_rows, LANES), f32),
            pltpu.VMEM((mode_rows, LANES), f32),
            pltpu.VMEM((mode_rows, LANES), f32),
            dma((3,)),
            dma((4,)),
            dma((2, seq_count)),
            dma((2, seq_count)),
            dma((3,)),
            dma((3,)),
            dma((2,)),
            dma((2,)),
            dma((seq_count // 2,)),
            dma((seq_count // 2,)),
            dma,
            dma,
        ],
        compiler_params=pltpu.CompilerParams(
            collective_id=0, has_side_effects=True, vmem_limit_bytes=60 * 1024 * 1024
        ),
    )(
        projected,
        short_taps,
        skip_gain.reshape(skip_gain.shape[0] // LANES, LANES),
        residue.T,
        decay_rate.T,
    )


def solution(mesh):
    in_specs = (P(None, "mp", "seq"), P(), P(), P("seq", None), P("seq", None))
    out_specs = P("mp", "seq")
    return jax.shard_map(body, mesh=mesh, in_specs=in_specs, out_specs=out_specs, check_vma=False)
```

```python
import functools

import jax
import jax.numpy as jnp
from jax import lax
from jax.experimental import pallas as pl
from jax.experimental.pallas import tpu as pltpu
from jax.sharding import PartitionSpec as P

MESH = pl.DeviceIdType.MESH
LANES = 128
ROWS = 8


def rows_of(first, count=ROWS):
    return pl.ds(pl.multiple_of(first, ROWS), count)


def kernel(
    seq_count,
    modes,
    half_count,
    length,
    filters,
    projected,
    taps_hbm,
    skip_hbm,
    residue_hbm,
    rate_hbm,
    out,
    residue,
    rate,
    streams,
    taps_raw,
    skip,
    taps,
    laid,
    product,
    mixed_q,
    local,
    own_params,
    params,
    rates,
    weights,
    decay,
    block_decay,
    pair_decay,
    halo_out,
    halo_in,
    own_state,
    mate_state,
    pair_state,
    states,
    carry,
    start,
    prefix,
    mate_prefix,
    in_sem,
    tap_sem,
    param_send,
    param_recv,
    halo_send,
    halo_recv,
    mate_send,
    mate_recv,
    state_send,
    state_recv,
    prefix_send,
    prefix_recv,
):
    me = lax.axis_index("seq")
    group = lax.axis_index("mp")
    block_count = half_count * ROWS
    width = block_count * LANES
    half_rows = length * ROWS
    mode_rows = modes * ROWS
    side = lax.rem(me, 2)
    pair = lax.div(me, 2)
    pair_count = seq_count // 2
    mate = me + 1 - 2 * side

    in_copies = [
        pltpu.make_async_copy(projected.at[s], streams.at[s], in_sem.at[s]) for s in range(3)
    ]
    tap_copy = pltpu.make_async_copy(
        taps_hbm.at[:, :, pl.ds(pl.multiple_of(group * width, LANES), width)],
        taps_raw,
        tap_sem.at[0],
    )
    skip_copy = pltpu.make_async_copy(
        skip_hbm.at[rows_of(group * block_count, block_count)], skip, tap_sem.at[1]
    )
    rate_copy = pltpu.make_async_copy(rate_hbm, rate, tap_sem.at[2])
    residue_copy = pltpu.make_async_copy(residue_hbm, residue, tap_sem.at[3])
    rate_copy.start()
    residue_copy.start()
    in_copies[1].start()
    tap_copy.start()
    in_copies[2].start()
    skip_copy.start()
    in_copies[0].start()

    def turn(s):
        in_copies[s].wait()
        for block in range(block_count):
            half, row = divmod(block, ROWS)
            laid[pl.ds((s * half_count + half) * half_rows + row, length, stride=ROWS), :] = (
                streams[s, block * LANES : (block + 1) * LANES, :].T.astype(jnp.float32)
            )

    barrier = pltpu.get_barrier_semaphore()

    def greet(step, _):
        peer = lax.rem(me + step, seq_count)
        pl.semaphore_signal(barrier, inc=1, device_id={"seq": peer}, device_id_type=MESH)
        return 0

    lax.fori_loop(1, seq_count, greet, 0)
    rate_copy.wait()
    residue_copy.wait()
    own_params[0] = rate[...]
    own_params[1] = residue[...] * jnp.sqrt(rate[...])
    params[me] = own_params[...]
    turn(1)
    tap_copy.wait()
    skip_copy.wait()
    for lag in range(3):
        for s in range(3):
            for block in range(block_count):
                taps[lag * 3 + s, block : block + 1, :] = taps_raw[
                    lag, s : s + 1, block * LANES : (block + 1) * LANES
                ]
    pl.semaphore_wait(barrier, seq_count - 1)

    def param_copy(kind, step):
        peer = lax.rem(me + step, seq_count)
        return pltpu.make_async_remote_copy(
            src_ref=own_params.at[kind],
            dst_ref=params.at[me, kind],
            send_sem=param_send.at[kind, step],
            recv_sem=param_recv.at[kind, step],
            device_id={"seq": peer},
            device_id_type=MESH,
        )

    def send_params(kind):
        first_side = 1 - lax.div(me, seq_count // 2)
        for target_side in (first_side, 1 - first_side):

            def send(ahead, _, target_side=target_side):
                peer = 2 * lax.rem(pair + ahead, pair_count) + target_side

                @pl.when(peer != me)
                def _():
                    param_copy(kind, lax.rem(peer - me + seq_count, seq_count)).start()

                return 0

            lax.fori_loop(0, pair_count, send, 0)

    send_params(0)

    def laid_row(s, half, t):
        return laid[rows_of((s * half_count + half) * half_rows + t * ROWS), :]

    turn(2)

    def halo_copy(s):
        return pltpu.make_async_remote_copy(
            src_ref=halo_out.at[s],
            dst_ref=halo_in.at[s],
            send_sem=halo_send.at[s],
            recv_sem=halo_recv.at[s],
            device_id={"seq": lax.rem(me + 1, seq_count)},
            device_id_type=MESH,
        )

    def send_halo(s):
        for back in range(2):
            pieces = [laid_row(s, half, length - 2 + back) for half in range(half_count)]
            halo_out[s, back] = jnp.concatenate(pieces, axis=0).astype(jnp.bfloat16)

        @pl.when(me < seq_count - 1)
        def _():
            halo_copy(s).start()

    def take_halo(s):
        @pl.when(me > 0)
        def _():
            halo_copy(s).wait_recv()

        @pl.when(me == 0)
        def _():
            halo_in[s] = jnp.zeros(halo_in.shape[1:], halo_in.dtype)

    send_halo(1)
    send_halo(2)
    turn(0)
    send_halo(0)
    send_params(1)
    def mix_streams(which, put):
        taps_of = [
            [
                [taps[lag * 3 + s, half * ROWS : (half + 1) * ROWS, :] for lag in range(3)]
                for s in which
            ]
            for half in range(half_count)
        ]

        def mix_at(half, t, now, before, earlier):
            put(
                rows_of(half * half_rows + t * ROWS),
                [
                    tap[0] * now[i] + tap[1] * before[i] + tap[2] * earlier[i]
                    for i, tap in enumerate(taps_of[half])
                ],
            )

        for half in range(half_count):

            def mix(t, past, half=half):
                before, earlier = past
                now = [laid_row(s, half, t) for s in which]
                mix_at(half, t, now, before, earlier)
                return now, before

            first = [[laid_row(s, half, t) for s in which] for t in range(2)]
            lax.fori_loop(2, length, mix, (first[1], first[0]), unroll=14)

        for s in which:
            take_halo(s)
        for half in range(half_count):
            past = [
                [
                    halo_in[s, back].astype(jnp.float32)[half * ROWS : (half + 1) * ROWS]
                    for s in which
                ]
                for back in range(2)
            ]
            first = [[laid_row(s, half, t) for s in which] for t in range(2)]
            mix_at(half, 0, first[0], past[1], past[0])
            mix_at(half, 1, first[1], first[0], past[1])

    def put_product(at, mixed):
        product[at, :] = (mixed[0] * mixed[1]).astype(jnp.bfloat16).astype(jnp.float32)

    def put_q(at, mixed):
        mixed_q[at, :] = mixed[0]

    mix_streams((1, 2), put_product)

    def take_params(kind, target, half):
        def take(sender, _):
            @pl.when(sender != me)
            def _():
                param_copy(kind, lax.rem(me - sender + seq_count, seq_count)).wait_recv()

            return 0

        first_sender = half * (seq_count // 2)
        lax.fori_loop(first_sender, first_sender + seq_count // 2, take, 0)
        for row in range(ROWS):
            if filters >= LANES:
                per = filters // LANES
                lane = (row % per) * LANES
                piece = params[first_sender + row // per, kind, :, lane : lane + LANES]
            else:
                per = LANES // filters
                piece = jnp.concatenate(
                    [params[first_sender + row * per + part, kind] for part in range(per)], axis=1
                )
            target[pl.ds(half * mode_rows + row, modes, stride=ROWS), :] = piece

    def of_modes(ref, half):
        first = half * mode_rows
        return [ref[rows_of(first + n * ROWS), :] for n in range(modes)]

    def find_state(half):
        here = rows_of(half * mode_rows, mode_rows)
        take_params(0, rates, half)
        decay[here, :] = jnp.exp(-rates[here, :])
        rate_of = of_modes(decay, half)

        def gather_state(t, held):
            value = product[rows_of(half * half_rows + t * ROWS), :]
            return [rate_of[n] * held[n] + value for n in range(modes)]

        held = lax.fori_loop(
            0,
            length,
            gather_state,
            [jnp.zeros((ROWS, LANES), jnp.float32)] * modes,
            unroll=16,
        )
        own_state[half] = jnp.concatenate(held, axis=0).astype(jnp.bfloat16)

    def mate_copy(half):
        return pltpu.make_async_remote_copy(
            src_ref=own_state.at[half],
            dst_ref=mate_state.at[half],
            send_sem=mate_send.at[half],
            recv_sem=mate_recv.at[half],
            device_id={"seq": mate},
            device_id_type=MESH,
        )

    find_state(1 - side)
    mate_copy(1 - side).start()
    find_state(side)

    @pl.when(side == 0)
    def _():
        mate_copy(0).start()

    def state_copy(sender, later):
        return pltpu.make_async_remote_copy(
            src_ref=pair_state,
            dst_ref=states.at[sender],
            send_sem=state_send.at[later],
            recv_sem=state_recv.at[sender],
            device_id={"seq": 2 * later + side},
            device_id_type=MESH,
        )

    def for_later(action):
        def step(later, _):
            action(state_copy(pair, later))
            return 0

        lax.fori_loop(pair + 1, pair_count, step, 0)

    block_decay[...] = jnp.exp(-float(length) * rates[...])
    pair_decay[...] = block_decay[...] * block_decay[...]
    mix_streams((0,), put_q)
    mate_copy(side).wait_recv()
    own_part = own_state[side].astype(jnp.float32)
    mate_part = mate_state[side].astype(jnp.float32)
    scale = block_decay[rows_of(side * mode_rows, mode_rows), :]
    even = jnp.where(side == 0, own_part, mate_part)
    odd = jnp.where(side == 0, mate_part, own_part)
    pair_state[...] = (scale * even + odd).astype(jnp.bfloat16)
    for_later(lambda copy: copy.start())
    for half in range(half_count):
        take_params(1, weights, half)

    start[...] = jnp.zeros(start.shape, jnp.float32)
    for half in (1, 0):

        @pl.when(side == 1)
        def _(half=half):
            if half == 0:
                mate_copy(0).wait_recv()
            start[...] = mate_state[half].astype(jnp.float32)

        rate_of = of_modes(decay, half)
        weight_of = of_modes(weights, half)

        def convolve(t, held, half=half, rate_of=rate_of, weight_of=weight_of):
            at = rows_of(half * half_rows + t * ROWS)
            value = product[at, :]
            held = [rate_of[n] * held[n] + value for n in range(modes)]
            local[at, :] = tree_sum([weight_of[n] * held[n] for n in range(modes)])
            return held

        lax.fori_loop(0, length, convolve, of_modes(start, 0), unroll=16)

    prefix_copy = pltpu.make_async_remote_copy(
        src_ref=prefix,
        dst_ref=mate_prefix,
        send_sem=prefix_send,
        recv_sem=prefix_recv,
        device_id={"seq": mate},
        device_id_type=MESH,
    )
    prefix[...] = jnp.zeros(prefix.shape, jnp.float32)

    def take_state(sender, _):
        state_copy(sender, sender).wait_recv()
        prefix[...] = prefix[...] * pair_decay[rows_of(side * mode_rows, mode_rows), :] + states[
            sender
        ].astype(jnp.float32)
        return 0

    lax.fori_loop(0, pair, take_state, 0)

    @pl.when(pair > 0)
    def _():
        prefix_copy.start()

    def put_gated(at, skip_here, long_part):
        long_part = long_part.astype(jnp.bfloat16).astype(jnp.float32)
        local[at, :] = mixed_q[at, :] * (long_part + skip_here * product[at, :])

    def gated_of(half, row):
        return local[pl.ds(half * half_rows + row, length, stride=ROWS), :].astype(jnp.bfloat16)

    def put_out(half, row, gated):
        first_channel = pl.multiple_of((half * ROWS + row) * LANES, LANES)
        out[pl.ds(first_channel, LANES), :] = gated.T

    @pl.when(pair == 0)
    def _():
        for half in range(half_count):
            skip_here = skip[rows_of(half * ROWS), :]

            def finish(t, _, half=half, skip_here=skip_here):
                at = rows_of(half * half_rows + t * ROWS)
                put_gated(at, skip_here, local[at, :])
                return 0

            lax.fori_loop(0, length, finish, 0, unroll=16)
            for row in range(ROWS):
                put_out(half, row, gated_of(half, row))

    @pl.when(pair > 0)
    def _():
        for order in range(2):
            half = side if order == 0 else 1 - side
            here = rows_of(half * mode_rows, mode_rows)
            if order == 0:
                carry[...] = prefix[...] * weights[here, :]
            else:
                prefix_copy.wait_recv()
                carry[...] = mate_prefix[...] * weights[here, :]

            @pl.when(side == 1)
            def _(here=here):
                carry[...] = carry[...] * block_decay[here, :]

            rate_of = of_modes(decay, half)
            skip_here = skip[rows_of(half * ROWS), :]

            def finish(t, held, half=half, rate_of=rate_of, skip_here=skip_here):
                at = rows_of(half * half_rows + t * ROWS)
                held = [rate_of[n] * held[n] for n in range(modes)]
                put_gated(at, skip_here, local[at, :] + tree_sum(held))
                return held

            lax.fori_loop(0, length, finish, of_modes(carry, 0), unroll=16)
            for row in range(ROWS):
                put_out(half, row, gated_of(half, row))

    def drain_params(step, _):
        for kind in range(2):
            param_copy(kind, step).wait_send()
        return 0

    lax.fori_loop(1, seq_count, drain_params, 0)

    @pl.when(me < seq_count - 1)
    def _():
        for s in range(3):
            halo_copy(s).wait_send()

    mate_copy(1 - side).wait_send()

    @pl.when(side == 0)
    def _():
        mate_copy(0).wait_send()

    for_later(lambda copy: copy.wait_send())

    @pl.when(pair > 0)
    def _():
        prefix_copy.wait_send()


def tree_sum(terms):
    while len(terms) > 1:
        terms = [terms[i] + terms[i + 1] for i in range(0, len(terms), 2)]
    return terms[0]


def body(projected, short_taps, skip_gain, residue, decay_rate):
    seq_count = lax.axis_size("seq")
    _, width, length = projected.shape
    filters, modes = residue.shape
    block_count = width // LANES
    half_count = block_count // ROWS
    assert half_count == 2 and seq_count % 2 == 0
    call = functools.partial(kernel, seq_count, modes, half_count, length, filters)
    hbm = pl.BlockSpec(memory_space=pltpu.HBM)
    mode_rows = modes * ROWS
    f32, bf16 = jnp.float32, jnp.bfloat16
    dma = pltpu.SemaphoreType.DMA
    return pl.pallas_call(
        call,
        out_shape=pltpu.VMEM((width, length), bf16),
        in_specs=[hbm] * 5,
        out_specs=pl.BlockSpec(memory_space=pltpu.VMEM),
        scratch_shapes=[
            pltpu.VMEM((modes, filters), f32),
            pltpu.VMEM((modes, filters), f32),
            pltpu.VMEM((3, width, length), bf16),
            pltpu.VMEM((3, 3, width), f32),
            pltpu.VMEM((block_count, LANES), f32),
            pltpu.VMEM((9, block_count, LANES), f32),
            pltpu.VMEM((3 * length * block_count, LANES), f32),
            pltpu.VMEM((length * block_count, LANES), f32),
            pltpu.VMEM((length * block_count, LANES), f32),
            pltpu.VMEM((length * block_count, LANES), f32),
            pltpu.VMEM((2, modes, filters), f32),
            pltpu.VMEM((seq_count, 2, modes, filters), f32),
            pltpu.VMEM((half_count * mode_rows, LANES), f32),
            pltpu.VMEM((half_count * mode_rows, LANES), f32),
            pltpu.VMEM((half_count * mode_rows, LANES), f32),
            pltpu.VMEM((half_count * mode_rows, LANES), f32),
            pltpu.VMEM((half_count * mode_rows, LANES), f32),
            pltpu.VMEM((3, 2, block_count, LANES), bf16),
            pltpu.VMEM((3, 2, block_count, LANES), bf16),
            pltpu.VMEM((half_count, mode_rows, LANES), bf16),
            pltpu.VMEM((half_count, mode_rows, LANES), bf16),
            pltpu.VMEM((mode_rows, LANES), bf16),
            pltpu.VMEM((seq_count // 2, mode_rows, LANES), bf16),
            pltpu.VMEM((mode_rows, LANES), f32),
            pltpu.VMEM((mode_rows, LANES), f32),
            pltpu.VMEM((mode_rows, LANES), f32),
            pltpu.VMEM((mode_rows, LANES), f32),
            dma((3,)),
            dma((4,)),
            dma((2, seq_count)),
            dma((2, seq_count)),
            dma((3,)),
            dma((3,)),
            dma((2,)),
            dma((2,)),
            dma((seq_count // 2,)),
            dma((seq_count // 2,)),
            dma,
            dma,
        ],
        compiler_params=pltpu.CompilerParams(
            collective_id=0, has_side_effects=True, vmem_limit_bytes=60 * 1024 * 1024
        ),
    )(
        projected,
        short_taps,
        skip_gain.reshape(skip_gain.shape[0] // LANES, LANES),
        residue.T,
        decay_rate.T,
    )


def solution(mesh):
    in_specs = (P(None, "mp", "seq"), P(), P(), P("seq", None), P("seq", None))
    out_specs = P("mp", "seq")
    return jax.shard_map(body, mesh=mesh, in_specs=in_specs, out_specs=out_specs, check_vma=False)
```
